512 devices in a mesh: section: 8 (over x_hi, y), tensor: 16 (over z), dp: 4 (over x_lo, core).
Axes of the slice: x: 4 (x_hi: 2, x_lo: 2; x = x_hi * 2 + x_lo), y: 4, z: 16, core: 2. Of those that a mesh axis runs over, the one named last changes fastest.
Arguments:
- activations: bfloat16 [512, 8, 8192], P('tensor', 'dp', 'section'), may hold values from -6 to 6
- old_heads: int32 [128], replicated, may hold values from 0 to 127, as said below
- new_heads: int32 [128], replicated, may hold values from 0 to 127, as said below
- xz_weight: bfloat16 [8192, 128, 128], P(('section', 'dp'), 'tensor'), may hold values from -0.0625 to 0.0625
- dt_weight: bfloat16 [8192, 128], P(('section', 'dp'), 'tensor'), may hold values from -0.0625 to 0.0625
- bc_weight: bfloat16 [8192, 2048], P('section', 'tensor'), may hold values from -0.0625 to 0.0625
- conv_heads: bfloat16 [128, 4, 64], P('tensor'), may hold values from -2.5 to 2.5
- conv_groups: bfloat16 [4, 2048], P(None, 'tensor'), may hold values from -2.5 to 2.5
- decay_log: bfloat16 [128], P('tensor'), may hold values from -5.5 to 1
- dt_bias: bfloat16 [128], P('tensor'), may hold values from -6 to -4
- skip_gain: bfloat16 [128], P('tensor'), may hold values from 0.5 to 1.5
- norm_gain: bfloat16 [128, 64], P('tensor'), may hold values from 0.5 to 1.5
- out_weight: bfloat16 [128, 64, 8192], P('tensor', None, ('section', 'dp')), may hold values from -0.0625 to 0.0625
Outputs:
- mixed: bfloat16 [512, 8, 8192], P(None, 'dp', 'section')
- relaid_xz: bfloat16 [8192, 128, 128], P(('section', 'dp'), 'tensor')
- relaid_out: bfloat16 [128, 64, 8192], P('tensor', None, ('section', 'dp'))
The draws below stay inside these ranges and needn't reach their ends.
Inputs may be any that keep to these rules, and one draw needn't show every extreme that they name: `old_heads`: a permutation of the head numbers. `new_heads`: a permutation of the head numbers; the heads of the old slots d * 8 .. (d+1) * 8 - 1 and of the new slots e * 8 .. (e+1) * 8 - 1 have at most 1 in common for any d and e, and exactly 1 for some pairs.
All inputs are finite; a program needn't handle non-finite values.
Results may differ from the reference program's by a relative error of at most 0.027.
Values may be sent and summed in bfloat16 or wider, within the bound.
A program may use at most 64 MiB of HBM per device.

```python
import jax
import jax.numpy as jnp
from jax import lax

D = 8192
HEADDIM = 64
STATE = 256
GROUP_HEADS = 32
HEAD_DEV = 8
KERNEL = 4
SEQ = 512
HEADS = 128
GROUPS = 4
BATCH = 8
N_SECTION = 8


def relay_maps(key):
    key_old, key_place, key_offset, key_order = jax.random.split(key, 4)
    owners = HEADS // HEAD_DEV
    old_heads = jax.random.permutation(key_old, HEADS).astype(jnp.int32)
    placing = jax.random.permutation(key_place, owners)
    offsets = jax.random.permutation(key_offset, owners)

    def one_order(subkey):
        return jax.random.permutation(subkey, HEAD_DEV)
    orders = jax.vmap(one_order)(jax.random.split(key_order, owners))
    source = jnp.arange(owners)[:, None]
    within = jnp.arange(HEAD_DEV)[None, :]
    target = placing[(source + offsets[within % owners]) % owners]
    slot_new = orders[target, within]
    flat_place = (target * HEAD_DEV + slot_new).reshape(-1)
    new_heads = jnp.zeros((HEADS,), jnp.int32).at[flat_place].set(old_heads)
    return (old_heads, new_heads)


def draw_old_heads(key, part):
    return relay_maps(key)[0]


def draw_new_heads(key, part):
    return relay_maps(key)[1]


def draw_decay_log(key, part):
    key = jax.random.fold_in(key, 7)
    values = jax.random.uniform(key, (HEADS,), jnp.float32, -4.0, 1.0)
    return values.astype(jnp.bfloat16)


def block_levels(stream_key, dims, cuts, least, largest):
    factor_of, own = 1.0, jax.random.fold_in(stream_key, 6)
    for axis_at, parts in cuts:
        steps = jnp.exp(jax.random.uniform(jax.random.fold_in(own, axis_at), (parts,), jnp.float32, least / len(cuts), largest / len(cuts)))
        factor_of = factor_of * jnp.repeat(steps, dims[axis_at] // parts).reshape([-1 if axis == axis_at else 1 for axis in range(len(dims))])
    return factor_of


def noise(stream_key, dims, spread, limit, cuts=(), kind=jnp.bfloat16):
    result = jax.random.normal(stream_key, dims, jnp.float32) * spread
    if len(cuts) > 0:
        result = block_levels(stream_key, dims, cuts, -0.22, 0.18) * result
    return jnp.clip(result, min=-limit, max=limit).astype(kind)


def setup_inputs(seed: int = 0) -> dict:
    splits = jax.random.split(jax.random.key(seed), 14)
    return {
        "activations": noise(splits[0], (SEQ, BATCH, D), 1.0, 6.0, ((0, 16), (1, 4), (2, 8))),
        "old_heads": draw_old_heads(jax.random.fold_in(splits[13], 71), 0),
        "new_heads": draw_new_heads(jax.random.fold_in(splits[13], 71), 0),
        "xz_weight": noise(splits[3], (D, HEADS, 2 * HEADDIM), D ** -0.5, 0.0625, ((0, 32), (1, 16))),
        "dt_weight": noise(splits[4], (D, HEADS), D ** -0.5, 0.0625, ((0, 32), (1, 16))),
        "bc_weight": noise(splits[5], (D, 2 * GROUPS * STATE), D ** -0.5, 0.0625, ((0, 8), (1, 16))),
        "conv_heads": noise(splits[6], (HEADS, KERNEL, HEADDIM), 0.5, 2.5, ((0, 16),)),
        "conv_groups": noise(splits[7], (KERNEL, 2 * GROUPS * STATE), 0.5, 2.5, ((1, 16),)),
        "decay_log": draw_decay_log(jax.random.fold_in(splits[13], 71), 0),
        "dt_bias": jnp.clip(-6.0 + 2.0 * jax.random.uniform(splits[9], (HEADS,), jnp.float32) ** block_levels(splits[9], (HEADS,), ((0, 16),), -0.2, 0.2), -6.0, -4.0).astype(jnp.bfloat16),
        "skip_gain": jnp.clip(0.5 + 1.0 * jax.random.uniform(splits[10], (HEADS,), jnp.float32) ** block_levels(splits[10], (HEADS,), ((0, 16),), -0.2, 0.2), 0.5, 1.5).astype(jnp.bfloat16),
        "norm_gain": jnp.clip(1.0 + 0.1 * jax.random.normal(splits[11], (HEADS, HEADDIM), jnp.float32), 0.5, 1.5).astype(jnp.bfloat16),
        "out_weight": noise(splits[12], (HEADS, HEADDIM, D), (HEADS * HEADDIM) ** -0.5, 0.0625, ((0, 16), (2, 32))),
    }


def rounded(value):
    return lax.optimization_barrier(value.astype(jnp.bfloat16)).astype(jnp.float32)

def reference(activations, old_heads, new_heads, xz_weight, dt_weight, bc_weight, conv_heads, conv_groups, decay_log, dt_bias, skip_gain, norm_gain, out_weight):
    numbers = jnp.arange(HEADS, dtype=jnp.int32)
    position = jnp.zeros((HEADS,), jnp.int32).at[old_heads].set(numbers)
    relay_index = jnp.take(position, new_heads, axis=0)
    relaid_xz = jnp.take(xz_weight, relay_index, axis=1)
    relaid_out = jnp.take(out_weight, relay_index, axis=0)
    canon_xz = jnp.take(xz_weight, position, axis=1)
    canon_dt = jnp.take(dt_weight, position, axis=1)
    canon_conv = jnp.take(conv_heads, position, axis=0).astype(jnp.float32)
    canon_decay = jnp.take(decay_log, position, axis=0).astype(jnp.float32)
    canon_bias = jnp.take(dt_bias, position, axis=0).astype(jnp.float32)
    canon_skip = jnp.take(skip_gain, position, axis=0).astype(jnp.float32)
    canon_gain = jnp.take(norm_gain, position, axis=0).astype(jnp.float32)
    canon_out = jnp.take(out_weight, position, axis=0)
    inner = HEADS * HEADDIM
    weights = jnp.concatenate([canon_xz.reshape(D, 2 * inner), canon_dt, bc_weight], axis=1)
    flattened = activations.reshape(SEQ * BATCH, D)
    width = D // N_SECTION

    def add_block(total, block):
        rows = lax.dynamic_slice_in_dim(flattened, block * width, width, 1)
        part = lax.dynamic_slice_in_dim(weights, block * width, width, 0)
        return (total + rounded(jnp.dot(rows, part, preferred_element_type=jnp.float32)), None)
    projected, _ = lax.scan(add_block, jnp.zeros((SEQ * BATCH, weights.shape[1]), jnp.float32), jnp.arange(N_SECTION, dtype=jnp.int32))
    xz_proj = projected[:, :2 * inner].reshape(SEQ, BATCH, HEADS, 2 * HEADDIM)
    raw_step = projected[:, 2 * inner:2 * inner + HEADS].reshape(SEQ, BATCH, HEADS)
    bc_raw = projected[:, 2 * inner + HEADS:].reshape(SEQ, BATCH, 2 * GROUPS * STATE)
    conv_in = jnp.concatenate([xz_proj[..., :HEADDIM].reshape(SEQ, BATCH, inner), bc_raw], axis=2)
    kernel = jnp.concatenate([jnp.transpose(canon_conv, (1, 0, 2)).reshape(KERNEL, inner), conv_groups.astype(jnp.float32)], axis=1)
    padded = jnp.pad(conv_in, ((KERNEL - 1, 0), (0, 0), (0, 0)))
    conv_sum = jnp.zeros_like(conv_in)
    for offset in range(KERNEL):
        conv_sum = conv_sum + kernel[offset] * padded[offset:offset + SEQ]
    convolved = jax.nn.silu(conv_sum).astype(jnp.bfloat16)
    x_values = convolved[..., :inner].astype(jnp.float32).reshape(SEQ, BATCH, HEADS, HEADDIM)
    bc_values = convolved[..., inner:].astype(jnp.float32).reshape(SEQ, BATCH, 2, GROUPS, STATE)
    step_size = jax.nn.softplus(raw_step + canon_bias)
    decay = jnp.exp(-step_size * jnp.exp(canon_decay))
    group_of = numbers // GROUP_HEADS

    def advance(state, inputs):
        decay_now, step_now, x_now, bc_now = inputs
        b_now = jnp.take(bc_now[:, 0], group_of, axis=1)
        c_now = jnp.take(bc_now[:, 1], group_of, axis=1)
        state = decay_now[:, :, None, None] * state + jnp.einsum('bhe,bhs->bhes', step_now[..., None] * x_now, b_now, precision=lax.Precision.HIGHEST)
        return (state, jnp.einsum('bhes,bhs->bhe', state, c_now, precision=lax.Precision.HIGHEST))
    start_state = jnp.zeros((BATCH, HEADS, HEADDIM, STATE), jnp.float32)
    _, scanned = lax.scan(advance, start_state, (decay, step_size, x_values, bc_values))
    y_values = scanned + canon_skip[:, None] * x_values
    gated = y_values * jax.nn.silu(xz_proj[..., HEADDIM:])
    squares = lax.optimization_barrier(jnp.sum(gated * gated, axis=3)).reshape(SEQ, BATCH, GROUPS, GROUP_HEADS).sum(axis=3)
    scale = lax.rsqrt(squares / (GROUP_HEADS * HEADDIM) + 1e-05)
    scale = jnp.repeat(scale, GROUP_HEADS, axis=2)
    normed = (gated * scale[..., None] * canon_gain).astype(jnp.bfloat16)
    total = jnp.dot(normed.reshape(SEQ * BATCH, inner), canon_out.reshape(inner, D), preferred_element_type=jnp.float32)
    mixed = (activations.astype(jnp.float32) + total.reshape(SEQ, BATCH, D)).astype(jnp.bfloat16)
    return (mixed, relaid_xz, relaid_out)
```

```python
import jax
import jax.numpy as jnp
from jax import lax
from jax.experimental import pallas as pl
from jax.experimental.pallas import tpu as pltpu
from jax.sharding import PartitionSpec as P

STATE = 256
GROUP_HEADS = 32
KERNEL = 4
MESH = pl.DeviceIdType.MESH
NZ, NS, ND = 16, 8, 4
VMEM = pl.BlockSpec(memory_space=pltpu.VMEM)
SMEM = pl.BlockSpec(memory_space=pltpu.SMEM)
F32, BF16 = jnp.float32, jnp.bfloat16
ARRIVAL = (0, -1, 1, -2, 2, -3, 3, -4, 4, -5, 5, -6, 6, -7, 7, -8)


def place():
    return lax.axis_index("section"), lax.axis_index("tensor"), lax.axis_index("dp")


def turn(index, by, size):
    return lax.rem(index + (by % size), size)


def greet(peers):
    barrier = pltpu.get_barrier_semaphore()
    for peer in peers:
        pl.semaphore_signal(barrier, inc=1, device_id=peer, device_id_type=MESH)
    pl.semaphore_wait(barrier, len(peers))


def send(source, target, send_sem, recv_sem, peer):
    copy = pltpu.make_async_remote_copy(
        src_ref=source,
        dst_ref=target,
        send_sem=send_sem,
        recv_sem=recv_sem,
        device_id=peer,
        device_id_type=MESH,
    )
    copy.start()
    return copy


def dims(lhs, rhs):
    return (((lhs,), (rhs,)), ((), ()))


def project_kernel(
    groups_ref, act_ref, xz_ref, dt_ref, bc_ref, out_ref, taps_ref,
    heads_out, steps_out, bc_out, rows_out,
    acts, weights, dts, parts, parts_in, bc_parts, bc_in, step_parts, steps_in,
    bc_all, chosen,
    w_send, w_recv, d_send, d_recv, o_send, o_recv, right_send, right_recv,
    left_send, left_recv, p_send, p_recv, b_send, b_recv, s_send, s_recv,
    z_send, z_recv, c_send, c_recv,
):
    s, t, d = place()
    right, left = (s, turn(t, 1, NZ), d), (s, turn(t, -1, NZ), d)
    sections = [turn(s, k, NS) for k in range(1, NS)]
    core = d + 1 - 2 * lax.rem(d, 2)
    across = turn(d, 2, ND)
    greet(
        [(s, turn(t, k, NZ), d) for k in range(1, NZ)]
        + [(p, t, d) for p in sections]
        + [(s, t, core), (s, t, across)]
    )
    sent = []

    def rows_at(index):
        return weights.at[pl.ds(pl.multiple_of(index * 256, 256), 256)]

    gathers = []
    for own, slot_of, ss, rs in (
        (xz_ref, rows_at, w_send, w_recv),
        (dt_ref, lambda i: dts.at[i], d_send, d_recv),
        (out_ref, lambda i: rows_out.at[i], o_send, o_recv),
    ):
        near = send(own, slot_of(d), ss.at[0], rs.at[0], (s, t, core))
        far = send(own, slot_of(d), ss.at[1], rs.at[1], (s, t, across))
        sent += [near, far]
        gathers.append((slot_of, ss, rs, near, far))

    def start_ring(c):
        rows = pl.ds(32 * c, 32)
        return [
            send(act_ref.at[rows], acts.at[t, rows], right_send.at[0, c], right_recv.at[0, c], right),
            send(act_ref.at[rows], acts.at[t, rows], left_send.at[0, c], left_recv.at[0, c], left),
        ]

    rings = [start_ring(0), start_ring(1)]
    sent += rings[0] + rings[1]
    acts[t] = act_ref[...]
    weights[pl.ds(pl.multiple_of(d * 256, 256), 256), :] = xz_ref[...]
    dts[d] = dt_ref[...]
    rows_out[d] = out_ref[...]

    forwarded = []

    def forward_weights():
        for slot_of, ss, rs, near, far in gathers:
            far.wait_recv()
            copy = send(slot_of(across), slot_of(across), ss.at[2], rs.at[2], (s, t, core))
            forwarded.append(copy)
            sent.append(copy)

    def have_weights():
        for (slot_of, ss, rs, near, far), copy in zip(gathers[:2], forwarded[:2]):
            near.wait_recv()
            copy.wait_recv()

    def block_of(i):
        return turn(t, ARRIVAL[i], NZ)

    part_copies = []

    def project(group):
        rows = jnp.concatenate([acts[block_of(4 * group + i)] for i in range(4)], axis=0)
        for half in range(2):
            product = jnp.dot(
                rows, weights[:, 512 * half : 512 * half + 512], preferred_element_type=F32
            ).astype(BF16)
            for j in range(4):
                parts[4 * half + j, 4 * group : 4 * group + 4] = product[
                    :, 128 * j : 128 * j + 128
                ].reshape(4, 64, 128)
        for k in range(1, NS):
            span = pl.ds(4 * group, 4)
            copy = send(
                parts.at[sections[k - 1], span],
                parts_in.at[k - 1, span],
                p_send.at[k - 1, group],
                p_recv.at[k - 1, group],
                (sections[k - 1], t, d),
            )
            part_copies.append(copy)
            sent.append(copy)

    for step in range(1, 9):
        for c in range(2):
            rows = pl.ds(32 * c, 32)
            rings[c][0].wait_recv()
            if step < 8:
                block = turn(t, -step, NZ)
                copy = send(
                    acts.at[block, rows], acts.at[block, rows],
                    right_send.at[step, c], right_recv.at[step, c], right,
                )
                rings[c][0] = copy
                sent.append(copy)
            if step < 8:
                rings[c][1].wait_recv()
            if step < 7:
                block = turn(t, step, NZ)
                copy = send(
                    acts.at[block, rows], acts.at[block, rows],
                    left_send.at[step, c], left_recv.at[step, c], left,
                )
                rings[c][1] = copy
                sent.append(copy)
        if step == 3:
            forward_weights()
        if step == 4:
            have_weights()
            project(0)
        if step == 5:
            project(1)
        if step == 6:
            project(2)

    bc_parts[0] = jnp.zeros((64, 128), BF16)
    for i in range(4):
        product = jnp.dot(
            acts[4 * i : 4 * i + 4].reshape(256, 1024), bc_ref[...], preferred_element_type=F32
        )
        bc_parts[1 + 4 * i : 5 + 4 * i] = product.astype(BF16).reshape(4, 64, 128)
    bc_copies = []
    for k in range(1, NS):
        copy = send(
            bc_parts.at[pl.ds(2 * sections[k - 1], 3)],
            bc_in.at[k - 1],
            b_send.at[k - 1],
            b_recv.at[k - 1],
            (sections[k - 1], t, d),
        )
        bc_copies.append(copy)
        sent.append(copy)
    project(3)
    raw = jnp.zeros((16, 1024), F32)
    for i in range(ND):
        raw = raw + lax.dot_general(
            dts[i],
            acts[:, :, 256 * i : 256 * i + 256].reshape(1024, 256),
            dims(1, 1),
            preferred_element_type=F32,
        )
    for j in range(NS):
        for r in range(8):
            step_parts[j, r : r + 1, :] = raw[j : j + 1, 128 * r : 128 * r + 128]
    step_copies = []
    for k in range(1, NS):
        copy = send(
            step_parts.at[sections[k - 1]],
            steps_in.at[k - 1],
            s_send.at[k - 1],
            s_recv.at[k - 1],
            (sections[k - 1], t, d),
        )
        step_copies.append(copy)
        sent.append(copy)

    for copy in bc_copies:
        copy.wait_recv()
    total = bc_parts[pl.ds(2 * s, 3)].astype(F32)
    for k in range(NS - 1):
        total = total + bc_in[k].astype(F32)
    for m in range(2):
        rows = total[:, 32 * m : 32 * m + 32, :].reshape(96, 128)
        u = jnp.zeros((64, 128), F32)
        for k in range(KERNEL):
            u = u + taps_ref[k : k + 1, :] * rows[29 + k : 93 + k]
        u = (u / (1.0 + jnp.exp(-u))).astype(BF16)
        bc_all[t, 32 * m : 32 * m + 32, :] = u[:32]
        bc_all[t, 64 + 32 * m : 96 + 32 * m, :] = u[32:]
    z_copies = []
    for k in range(1, NZ):
        copy = send(
            bc_all.at[t], bc_all.at[t], z_send.at[k - 1], z_recv.at[k - 1], (s, turn(t, k, NZ), d)
        )
        z_copies.append(copy)
        sent.append(copy)
    for copy in z_copies:
        copy.wait_recv()

    def choose(section, j):
        return bc_all[8 * (j // 2) + 2 * groups_ref[section] + j % 2]

    choice_copies = []
    for k in range(1, NS):
        for j in range(4):
            chosen[k - 1, j] = choose(sections[k - 1], j)
        copy = send(
            chosen.at[k - 1], bc_out.at[s], c_send.at[k - 1], c_recv.at[k - 1],
            (sections[k - 1], t, d),
        )
        choice_copies.append(copy)
        sent.append(copy)
    for j in range(4):
        bc_out[s, j] = choose(s, j)

    for copy in part_copies + step_copies:
        copy.wait_recv()
    for i in range(NZ):
        value = parts[s, i].astype(F32)
        for k in range(NS - 1):
            value = value + parts_in[k, i].astype(F32)
        heads_out[block_of(i)] = value
    value = step_parts[s]
    for k in range(NS - 1):
        value = value + steps_in[k]
    steps_out[...] = value

    gathers[2][3].wait_recv()
    forwarded[2].wait_recv()
    for copy in choice_copies:
        copy.wait_recv()
    for copy in sent:
        copy.wait_send()


def project_call(groups, act, xz, dt, bc, out, taps):
    dma = pltpu.SemaphoreType.DMA
    return pl.pallas_call(
        project_kernel,
        out_shape=(
            jax.ShapeDtypeStruct((NZ, 64, 128), F32),
            jax.ShapeDtypeStruct((8, 128), F32),
            jax.ShapeDtypeStruct((NS, 4, 128, 128), BF16),
            jax.ShapeDtypeStruct((ND, 512, 256), BF16),
        ),
        in_specs=[SMEM] + [VMEM] * 6,
        out_specs=(VMEM,) * 4,
        scratch_shapes=[
            pltpu.VMEM((NZ, 64, 1024), BF16),
            pltpu.VMEM((1024, 1024), BF16),
            pltpu.VMEM((ND, 16, 256), BF16),
            pltpu.VMEM((NS, NZ, 64, 128), BF16),
            pltpu.VMEM((NS - 1, NZ, 64, 128), BF16),
            pltpu.VMEM((NZ + 1, 64, 128), BF16),
            pltpu.VMEM((NS - 1, 3, 64, 128), BF16),
            pltpu.VMEM((NS, 8, 128), F32),
            pltpu.VMEM((NS - 1, 8, 128), F32),
            pltpu.VMEM((NZ, 128, 128), BF16),
            pltpu.VMEM((NS - 1, 4, 128, 128), BF16),
            dma((3,)), dma((3,)), dma((3,)), dma((3,)), dma((3,)), dma((3,)),
            dma((8, 2)), dma((8, 2)), dma((8, 2)), dma((8, 2)),
            dma((NS - 1, 4)), dma((NS - 1, 4)),
            dma((NS - 1,)), dma((NS - 1,)), dma((NS - 1,)), dma((NS - 1,)),
            dma((NZ - 1,)), dma((NZ - 1,)), dma((NS - 1,)), dma((NS - 1,)),
        ],
        compiler_params=pltpu.CompilerParams(
            collective_id=0, has_side_effects=True, vmem_limit_bytes=40 << 20
        ),
        cost_estimate=pl.CostEstimate(
            flops=3_000_000_000, bytes_accessed=100_000_000, transcendentals=0
        ),
    )(groups, act, xz, dt, bc, out, taps)


def scan_kernel(heads_ref, step_ref, log_ref, bc_ref, taps_ref, gated_out):
    lane = lax.broadcasted_iota(jnp.int32, (128, 128), 1)
    row = lax.broadcasted_iota(jnp.int32, (128, 128), 0)
    causal = row >= lane
    upto = (row <= lane).astype(F32)
    same = (row == lane).astype(F32)
    exact = lax.Precision.HIGHEST
    cum = jnp.dot(log_ref[...], upto, precision=exact, preferred_element_type=F32)
    step = step_ref[...]
    both = jnp.concatenate([cum, step], axis=0)
    columns = lax.dot_general(same, both, dims(1, 1), precision=exact, preferred_element_type=F32)
    tall = lax.broadcasted_iota(jnp.int32, (512, 128), 0)
    gated = []
    for m in range(2):
        v = heads_ref[:, 32 * m : 32 * m + 32, :].reshape(512, 128)
        u = taps_ref[3:4, :] * v
        for back in range(1, KERNEL):
            moved = jnp.where(tall >= back, pltpu.roll(v, back, 0), 0.0)
            u = u + taps_ref[3 - back : 4 - back, :] * moved
        x = (u / (1.0 + jnp.exp(-u))).astype(BF16)
        state = jnp.zeros((STATE, 128), F32)
        outs = []
        for c in range(4):
            at = 4 * m + c

            def pick(j):
                part = bc_ref[2 * c : 2 * c + 2, j].reshape(2, 2, 2, 32, 128)
                return part[:, :, m].reshape(128, 128)

            b = jnp.concatenate([pick(0), pick(1)], axis=1)
            cc = jnp.concatenate([pick(2), pick(3)], axis=1)
            xc = x[128 * c : 128 * c + 128]
            xf = xc.astype(F32)
            cum_c, step_c = columns[:, at : at + 1], columns[:, 8 + at : 9 + at]
            cum_r, step_r = cum[at : at + 1, :], step[at : at + 1, :]
            scores = lax.dot_general(cc, b, dims(1, 1), preferred_element_type=F32)
            mixing = jnp.exp(jnp.where(causal, cum_c - cum_r, -1e30)) * step_r
            y = jnp.dot((scores * mixing).astype(BF16), xc, preferred_element_type=F32)
            y = y + jnp.exp(cum_c) * jnp.dot(cc, state.astype(BF16), preferred_element_type=F32)
            y = y + taps_ref[4:5, :] * xf
            outs.append(y)
            if c < 3:
                end = cum[at : at + 1, 127:128]
                tail = (jnp.exp(end - cum_c) * step_c * xf).astype(BF16)
                state = jnp.exp(end) * state + lax.dot_general(
                    b, tail, dims(0, 0), preferred_element_type=F32
                )
        z = pltpu.roll(v, 64, 1)
        gated.append(jnp.concatenate(outs, axis=0) * (z / (1.0 + jnp.exp(-z))))
    wide = lax.broadcasted_iota(jnp.int32, (512, 128), 1)
    gated_out[...] = jnp.where(wide < 64, gated[0], pltpu.roll(gated[1], 64, 1)).astype(BF16)


def scan_call(heads, step, log_decay, bc, taps):
    return pl.pallas_call(
        scan_kernel,
        out_shape=jax.ShapeDtypeStruct((512, 128), BF16),
        in_specs=[VMEM] * 5,
        out_specs=VMEM,
        compiler_params=pltpu.CompilerParams(vmem_limit_bytes=32 << 20),
        cost_estimate=pl.CostEstimate(
            flops=200_000_000, bytes_accessed=3_000_000, transcendentals=500_000
        ),
    )(heads, step, log_decay, bc, taps)


def mix_kernel(
    gated_ref, rows_ref, act_ref, hot_ref, gain_ref,
    mixed_out,
    gathered, squares, squares_in, totals, product, right_out, right_in, left_out, left_in,
    g_send, g_recv, q_send, q_recv, y_send, y_recv,
    right_send, right_recv, left_send, left_recv,
    gr_send, gr_recv, gl_send, gl_recv,
):
    s, t, d = place()
    right, left = (s, turn(t, 1, NZ), d), (s, turn(t, -1, NZ), d)
    sections = [turn(s, k, NS) for k in range(1, NS)]
    y = lax.rem(s, 4)
    columns = [s - y + turn(y, k, 4) for k in range(1, 4)]
    greet([(s, turn(t, k, NZ), d) for k in range(1, NZ)] + [(p, t, d) for p in sections])
    sent = []

    copies = []
    for k in range(1, NS):
        copy = send(
            gated_ref, gathered.at[s], g_send.at[k - 1], g_recv.at[k - 1], (sections[k - 1], t, d)
        )
        copies.append(copy)
    gathered[s] = gated_ref[...]
    sent += copies
    for copy in copies:
        copy.wait_recv()

    for j in range(4):
        value = jnp.zeros((8, 128), F32)
        for i in range(NS):
            part = gathered[i, 128 * j : 128 * j + 128, :].astype(F32)
            value = value + lax.dot_general(
                hot_ref[:8, 128 * i : 128 * i + 128],
                (part * part).astype(BF16),
                dims(1, 1),
                preferred_element_type=F32,
            )
        squares[j] = value
    copies = []
    for k in range(1, NZ):
        copy = send(
            squares.at[y], squares_in.at[k - 1], q_send.at[k - 1], q_recv.at[k - 1],
            (s, turn(t, k, NZ), d),
        )
        copies.append(copy)
    sent += copies
    for copy in copies:
        copy.wait_recv()
    value = squares[y]
    for k in range(NZ - 1):
        value = value + squares_in[k]
    totals[y] = value
    copies = []
    for k in range(3):
        copy = send(
            totals.at[y], totals.at[y], y_send.at[k], y_recv.at[k], (columns[k], t, d)
        )
        copies.append(copy)
    sent += copies
    for copy in copies:
        copy.wait_recv()

    wide = lax.broadcasted_iota(jnp.int32, (128, 128), 1)
    for j in range(4):
        inverse = lax.rsqrt(totals[j] / (GROUP_HEADS * 64) + 1e-05)
        high = inverse.astype(BF16)
        low = (inverse - high.astype(F32)).astype(BF16)
        scale = lax.dot_general(
            jnp.concatenate([high, low], axis=0), hot_ref[...], dims(0, 0),
            preferred_element_type=F32,
        )
        first, second = [], []
        for i in range(0, NS, 2):
            pair = []
            for h in (i, i + 1):
                span = slice(128 * h, 128 * h + 128)
                value = gathered[h, 128 * j : 128 * j + 128, :].astype(F32)
                pair.append(value * scale[:, span] * gain_ref[0:1, span])
            even, odd = pair
            first.append(jnp.where(wide < 64, even, pltpu.roll(odd, 64, 1)).astype(BF16))
            second.append(jnp.where(wide < 64, pltpu.roll(even, 64, 1), odd).astype(BF16))
        lhs = jnp.concatenate(
            [jnp.concatenate(first, axis=1), jnp.concatenate(second, axis=1)], axis=0
        )
        for i in range(ND):
            result = jnp.dot(lhs, rows_ref[i], preferred_element_type=F32)
            for m in range(2):
                product[
                    4 * j : 4 * j + 4, 32 * m : 32 * m + 32, 256 * i : 256 * i + 256
                ] = result[128 * m : 128 * m + 128].reshape(4, 32, 256)

    from_left, from_right = [None, None], [None, None]
    for step in range(8):
        for h in range(2):
            span = slice(512 * h, 512 * h + 512)
            value = product[turn(t, 8 - step, NZ), :, span]
            if step > 0:
                from_left[h].wait_recv()
                value = value + right_in[step - 1, h].astype(F32)
            right_out[step, h] = value.astype(BF16)
            from_left[h] = send(
                right_out.at[step, h], right_in.at[step, h],
                right_send.at[step, h], right_recv.at[step, h], right,
            )
            sent.append(from_left[h])
            if step < 7:
                value = product[turn(t, step - 7, NZ), :, span]
                if step > 0:
                    from_right[h].wait_recv()
                    value = value + left_in[step - 1, h].astype(F32)
                left_out[step, h] = value.astype(BF16)
                from_right[h] = send(
                    left_out.at[step, h], left_in.at[step, h],
                    left_send.at[step, h], left_recv.at[step, h], left,
                )
                sent.append(from_right[h])
    for h in range(2):
        span = slice(512 * h, 512 * h + 512)
        from_left[h].wait_recv()
        from_right[h].wait_recv()
        value = product[t, :, span] + act_ref[:, span].astype(F32)
        value = value + right_in[7, h].astype(F32) + left_in[6, h].astype(F32)
        mixed_out[t, :, span] = value.astype(BF16)

    rings = [[None, None], [None, None]]
    for step in range(9):
        for c in range(2):
            rows = pl.ds(32 * c, 32)
            if step > 0:
                rings[c][0].wait_recv()
            if step < 8:
                block = turn(t, -step, NZ)
                rings[c][0] = send(
                    mixed_out.at[block, rows], mixed_out.at[block, rows],
                    gr_send.at[step, c], gr_recv.at[step, c], right,
                )
                sent.append(rings[c][0])
            if 0 < step < 8:
                rings[c][1].wait_recv()
            if step < 7:
                block = turn(t, step, NZ)
                rings[c][1] = send(
                    mixed_out.at[block, rows], mixed_out.at[block, rows],
                    gl_send.at[step, c], gl_recv.at[step, c], left,
                )
                sent.append(rings[c][1])
    for copy in sent:
        copy.wait_send()


def mix_call(gated, rows, act, hot, gain):
    dma = pltpu.SemaphoreType.DMA
    return pl.pallas_call(
        mix_kernel,
        out_shape=jax.ShapeDtypeStruct((NZ, 64, 1024), BF16),
        in_specs=[VMEM] * 5,
        out_specs=VMEM,
        scratch_shapes=[
            pltpu.VMEM((NS, 512, 128), BF16),
            pltpu.VMEM((4, 8, 128), F32),
            pltpu.VMEM((NZ - 1, 8, 128), F32),
            pltpu.VMEM((4, 8, 128), F32),
            pltpu.VMEM((NZ, 64, 1024), F32),
            pltpu.VMEM((8, 2, 64, 512), BF16),
            pltpu.VMEM((8, 2, 64, 512), BF16),
            pltpu.VMEM((7, 2, 64, 512), BF16),
            pltpu.VMEM((7, 2, 64, 512), BF16),
            dma((NS - 1,)), dma((NS - 1,)), dma((NZ - 1,)), dma((NZ - 1,)), dma((3,)), dma((3,)),
            dma((8, 2)), dma((8, 2)), dma((7, 2)), dma((7, 2)),
            dma((8, 2)), dma((8, 2)), dma((7, 2)), dma((7, 2)),
        ],
        compiler_params=pltpu.CompilerParams(
            collective_id=1, has_side_effects=True, vmem_limit_bytes=40 << 20
        ),
        cost_estimate=pl.CostEstimate(
            flops=1_100_000_000, bytes_accessed=100_000_000, transcendentals=0
        ),
    )(gated, rows, act, hot, gain)


def relay(old_heads, new_heads, xz_weight, out_weight):
    owners = lax.axis_size("tensor")
    member = lax.axis_index("tensor")
    head_dev = xz_weight.shape[1]
    mine_old = lax.dynamic_slice_in_dim(old_heads, member * head_dev, head_dev)
    mine_new = lax.dynamic_slice_in_dim(new_heads, member * head_dev, head_dev)
    numbers = jnp.arange(old_heads.shape[0], dtype=jnp.int32)
    position = jnp.sum(
        jnp.where(new_heads[None, :] == mine_old[:, None], numbers[None, :], 0), axis=1
    )
    origin = jnp.sum(
        jnp.where(old_heads[None, :] == mine_new[:, None], numbers[None, :], 0), axis=1
    )
    devices = jnp.arange(owners, dtype=jnp.int32)
    chosen = (position[None, :] // head_dev == devices[:, None]).astype(BF16)
    placing = (origin[None, :] // head_dev == devices[:, None]).astype(BF16)

    def select(form, mask, array):
        return jnp.einsum(form, mask, array, preferred_element_type=F32).astype(BF16)

    def exchange(array):
        return lax.all_to_all(array, "tensor", split_axis=0, concat_axis=0, tiled=True)

    moved_xz = exchange(select("dj,rjq->drq", chosen, xz_weight))
    moved_out = exchange(select("dj,jer->der", chosen, out_weight))
    new_xz = select("sk,srq->rkq", placing, moved_xz)
    new_out = select("sk,ser->ker", placing, moved_out)
    return new_xz, new_out


def per_device(
    activations,
    old_heads,
    new_heads,
    xz_weight,
    dt_weight,
    bc_weight,
    conv_heads,
    conv_groups,
    decay_log,
    dt_bias,
    skip_gain,
    norm_gain,
    out_weight,
):
    s, t, _ = place()
    head_dev = xz_weight.shape[1]
    groups = lax.dynamic_slice_in_dim(old_heads, t * head_dev, head_dev) // GROUP_HEADS
    act = jnp.transpose(activations, (1, 0, 2)).reshape(64, 1024)
    step_rows = jnp.pad(jnp.transpose(dt_weight), ((0, 8), (0, 0)))
    heads, raw, bc, rows = project_call(
        groups,
        act,
        xz_weight.reshape(256, 1024),
        step_rows,
        bc_weight,
        out_weight.reshape(512, 256),
        jnp.pad(conv_groups.astype(F32), ((0, 4), (0, 0))),
    )

    def own(array):
        return lax.dynamic_index_in_dim(array, s, 0, keepdims=False).astype(F32)

    raw = jnp.transpose(raw.reshape(4, 4, 2, 32), (2, 0, 1, 3)).reshape(8, 128)
    step = jax.nn.softplus(raw + own(dt_bias))
    log_decay = -step * jnp.exp(own(decay_log))
    taps = own(conv_heads)
    taps = jnp.concatenate([taps, taps], axis=1)
    skip = jnp.broadcast_to(own(skip_gain), (4, 128))
    gated = scan_call(heads, step, log_decay, bc, jnp.concatenate([taps, skip], axis=0))

    index = jnp.arange(8, dtype=jnp.int32)
    hot = (
        (index[:, None, None] % 4 == groups[None, :, None])
        & (index[:, None, None] // 4 == jnp.arange(2, dtype=jnp.int32)[None, None, :])
    ).astype(BF16)
    hot = jnp.broadcast_to(hot[:, :, :, None], (8, 8, 2, 64)).reshape(8, 1024)
    hot = jnp.concatenate([hot, hot], axis=0)
    gain = jnp.broadcast_to(norm_gain.astype(F32)[:, None, :], (8, 2, 64)).reshape(1, 1024)
    gain = jnp.broadcast_to(gain, (8, 1024))
    mixed = mix_call(gated, rows, act, hot, gain)
    mixed = jnp.transpose(mixed.reshape(16, 2, 32, 1024), (0, 2, 1, 3)).reshape(512, 2, 1024)
    new_xz, new_out = relay(old_heads, new_heads, xz_weight, out_weight)
    return mixed, new_xz, new_out


def solution(mesh):
    in_specs = (
        P("tensor", "dp", "section"),
        P(),
        P(),
        P(("section", "dp"), "tensor", None),
        P(("section", "dp"), "tensor"),
        P("section", "tensor"),
        P("tensor", None, None),
        P(None, "tensor"),
        P("tensor"),
        P("tensor"),
        P("tensor"),
        P("tensor", None),
        P("tensor", None, ("section", "dp")),
    )
    out_specs = (
        P(None, "dp", "section"),
        P(("section", "dp"), "tensor", None),
        P("tensor", None, ("section", "dp")),
    )
    return jax.shard_map(
        per_device, mesh=mesh, in_specs=in_specs, out_specs=out_specs, check_vma=False
    )
```

```python
import jax
import jax.numpy as jnp
from jax import lax
from jax.experimental import pallas as pl
from jax.experimental.pallas import tpu as pltpu
from jax.sharding import PartitionSpec as P

STATE = 256
GROUP_HEADS = 32
KERNEL = 4
MESH = pl.DeviceIdType.MESH
NZ, NS, ND = 16, 8, 4
CHUNKS = 4
ROWS, WIDTH = 64 // CHUNKS, 1024 // CHUNKS
EARLY = (1, -1, 2, -2)
LATE = (3, -3, 4, -4, 5, -5, 6, -6, 7, -7, 8)
VMEM = pl.BlockSpec(memory_space=pltpu.VMEM)
SMEM = pl.BlockSpec(memory_space=pltpu.SMEM)
F32, BF16 = jnp.float32, jnp.bfloat16
ARRIVAL = (0, -1, 1, -2, 2, -3, 3, -4, 4, -5, 5, -6, 6, -7, 7, -8)


def place():
    return lax.axis_index("section"), lax.axis_index("tensor"), lax.axis_index("dp")


def turn(index, by, size):
    return lax.rem(index + (by % size), size)


def greet(peers):
    barrier = pltpu.get_barrier_semaphore()
    for peer in peers:
        pl.semaphore_signal(barrier, inc=1, device_id=peer, device_id_type=MESH)
    pl.semaphore_wait(barrier, len(peers))


def send(source, target, send_sem, recv_sem, peer):
    copy = pltpu.make_async_remote_copy(
        src_ref=source,
        dst_ref=target,
        send_sem=send_sem,
        recv_sem=recv_sem,
        device_id=peer,
        device_id_type=MESH,
    )
    copy.start()
    return copy


def dims(lhs, rhs):
    return (((lhs,), (rhs,)), ((), ()))


def layer_kernel(
    groups_ref, reads_ref, leaving_ref, origin_ref, scalars_ref,
    act_ref, xz_ref, dt_ref, bc_ref, out_ref, group_taps_ref, head_taps_ref, gain_ref,
    mixed_out, new_xz, new_rows,
    hot_ref, acts, weights, dts, rows_all, parts, parts_in, bc_parts, bc_in, step_parts, steps_in,
    bc_all, chosen, groups_in, xz_leaving, xz_coming, rows_leaving, rows_coming,
    own_gated, gathered, own_squares, squares_in, squares, z_squares, totals, product,
    right_out, right_in, left_out, left_in,
    w_send, w_recv, d_send, d_recv, o_send, o_recv, right_send, right_recv,
    left_send, left_recv, p_send, p_recv, b_send, b_recv, s_send, s_recv,
    z_send, z_recv, c_send, c_recv, e_send, e_recv, f_send, f_recv,
    g_send, g_recv, q_send, q_recv, u_send, u_recv, y_send, y_recv,
    sr_send, sr_recv, sl_send, sl_recv, gr_send, gr_recv, gl_send, gl_recv,
):
    s, t, d = place()
    right, left = (s, turn(t, 1, NZ), d), (s, turn(t, -1, NZ), d)
    sections = [turn(s, k, NS) for k in range(1, NS)]
    core = d + 1 - 2 * lax.rem(d, 2)
    across = turn(d, 2, ND)
    greet(
        [(s, turn(t, k, NZ), d) for k in range(1, NZ)]
        + [(p, t, d) for p in sections]
        + [(s, t, core), (s, t, across)]
    )
    sent = []

    def rows_at(index):
        return weights.at[pl.ds(pl.multiple_of(index * 256, 256), 256)]

    gathers = []

    def give(own, slot_of, ss, rs):
        near = send(own, slot_of(d), ss.at[0], rs.at[0], (s, t, core))
        far = send(own, slot_of(d), ss.at[1], rs.at[1], (s, t, across))
        sent.extend([near, far])
        gathers.append((slot_of, ss, rs, near, far))

    def start_ring(c):
        rows = pl.ds(ROWS * c, ROWS)
        return [
            send(act_ref.at[rows], acts.at[t, rows], right_send.at[0, c], right_recv.at[0, c], right),
            send(act_ref.at[rows], acts.at[t, rows], left_send.at[0, c], left_recv.at[0, c], left),
        ]

    rings = [start_ring(c) for c in range(CHUNKS)]
    for ring in rings:
        sent.extend(ring)
    own_rows = pl.ds(pl.multiple_of(d * 256, 256), 256)
    for h in range(NS):
        weights[own_rows, 128 * h : 128 * h + 128] = xz_ref[h]
    give(rows_at(d), rows_at, w_send, w_recv)
    give(dt_ref, lambda i: dts.at[i], d_send, d_recv)
    acts[t] = act_ref[...]
    dts[d] = dt_ref[...]
    rows_all[d] = out_ref[...].reshape(512, 256)
    lane = lax.broadcasted_iota(jnp.int32, (16, 128), 1)
    row = lax.rem(lax.broadcasted_iota(jnp.int32, (16, 128), 0), 8)
    halves = jnp.where(lane < 64, 0, 4)
    for h in range(NS):
        hot_ref[:, 128 * h : 128 * h + 128] = (row == halves + groups_ref[h]).astype(F32).astype(BF16)

    def pack(k):
        there = turn(t, k, NZ)
        if k == 0:
            xz_coming[t] = xz_ref[leaving_ref[there]]
            rows_coming[t] = out_ref[leaving_ref[there]]
        else:
            xz_leaving[k - 1] = xz_ref[leaving_ref[there]]
            rows_leaving[k - 1] = out_ref[leaving_ref[there]]

    for k in range(NZ):
        pack(k)
    moves = []

    def move(k):
        there = (s, turn(t, k, NZ), d)
        for source, target, ss, rs in (
            (xz_leaving, xz_coming, e_send, e_recv),
            (rows_leaving, rows_coming, f_send, f_recv),
        ):
            copy = send(source.at[k - 1], target.at[t], ss.at[k - 1], rs.at[k - 1], there)
            moves.append(copy)
            sent.append(copy)

    forwarded = []

    def forward_weights(which):
        slot_of, ss, rs, near, far = gathers[which]
        far.wait_recv()
        copy = send(slot_of(across), slot_of(across), ss.at[2], rs.at[2], (s, t, core))
        forwarded.append(copy)
        sent.append(copy)

    def have_weights(which):
        gathers[which][3].wait_recv()
        forwarded[which].wait_recv()

    def block_of(i):
        return turn(t, ARRIVAL[i], NZ)

    part_copies = []

    def project(group):
        rows = jnp.concatenate([acts[block_of(4 * group + i)] for i in range(4)], axis=0)
        for half in range(2):
            result = jnp.dot(
                rows, weights[:, 512 * half : 512 * half + 512], preferred_element_type=F32
            ).astype(BF16)
            for j in range(4):
                parts[4 * half + j, 4 * group : 4 * group + 4] = result[
                    :, 128 * j : 128 * j + 128
                ].reshape(4, 64, 128)
        for k in range(1, NS):
            span = pl.ds(4 * group, 4)
            copy = send(
                parts.at[sections[k - 1], span],
                parts_in.at[k - 1, span],
                p_send.at[k - 1, group],
                p_recv.at[k - 1, group],
                (sections[k - 1], t, d),
            )
            part_copies.append(copy)
            sent.append(copy)

    for step in range(1, 9):
        for c in range(CHUNKS):
            rows = pl.ds(ROWS * c, ROWS)
            rings[c][0].wait_recv()
            if step < 8:
                block = turn(t, -step, NZ)
                copy = send(
                    acts.at[block, rows], acts.at[block, rows],
                    right_send.at[step, c], right_recv.at[step, c], right,
                )
                rings[c][0] = copy
                sent.append(copy)
            if step < 8:
                rings[c][1].wait_recv()
            if step < 7:
                block = turn(t, step, NZ)
                copy = send(
                    acts.at[block, rows], acts.at[block, rows],
                    left_send.at[step, c], left_recv.at[step, c], left,
                )
                rings[c][1] = copy
                sent.append(copy)
        if step == 3:
            forward_weights(0)
            forward_weights(1)
        if step == 4:
            have_weights(0)
            have_weights(1)
            project(0)
        if step == 5:
            project(1)
        if step == 6:
            project(2)

    bc_parts[0] = jnp.zeros((64, 128), BF16)
    for i in range(4):
        result = jnp.dot(
            acts[4 * i : 4 * i + 4].reshape(256, 1024), bc_ref[...], preferred_element_type=F32
        )
        bc_parts[1 + 4 * i : 5 + 4 * i] = result.astype(BF16).reshape(4, 64, 128)
    bc_copies = []
    for k in range(1, NS):
        copy = send(
            bc_parts.at[pl.ds(2 * sections[k - 1], 3)],
            bc_in.at[k - 1],
            b_send.at[k - 1],
            b_recv.at[k - 1],
            (sections[k - 1], t, d),
        )
        bc_copies.append(copy)
        sent.append(copy)
    for k in EARLY:
        move(k % NZ)
    project(3)
    raw = jnp.zeros((16, 1024), F32)
    for i in range(ND):
        raw = raw + lax.dot_general(
            dts[i],
            acts[:, :, 256 * i : 256 * i + 256].reshape(1024, 256),
            dims(1, 1),
            preferred_element_type=F32,
        )
    for j in range(NS):
        for r in range(8):
            step_parts[j, r : r + 1, :] = raw[j : j + 1, 128 * r : 128 * r + 128]
    step_copies = []
    for k in range(1, NS):
        copy = send(
            step_parts.at[sections[k - 1]],
            steps_in.at[k - 1],
            s_send.at[k - 1],
            s_recv.at[k - 1],
            (sections[k - 1], t, d),
        )
        step_copies.append(copy)
        sent.append(copy)

    for copy in bc_copies:
        copy.wait_recv()
    total = bc_parts[pl.ds(2 * s, 3)].astype(F32)
    for k in range(NS - 1):
        total = total + bc_in[k].astype(F32)
    own_class, own_turn = 4 * lax.rem(t, 4), t // 4
    taps = group_taps_ref[...].astype(F32)
    for m in range(2):
        rows = total[:, 32 * m : 32 * m + 32, :].reshape(96, 128)
        u = jnp.zeros((64, 128), F32)
        for k in range(KERNEL):
            u = u + taps[k : k + 1, :] * rows[29 + k : 93 + k]
        u = (u / (1.0 + jnp.exp(-u))).astype(BF16)
        bc_all[own_class + own_turn, 32 * m : 32 * m + 32, :] = u[:32]
        bc_all[own_class + own_turn, 64 + 32 * m : 96 + 32 * m, :] = u[32:]

    def spread(copies, source, slot, by):
        copy = send(source, source, z_send.at[slot], z_recv.at[slot], (s, turn(t, by, NZ), d))
        copies.append(copy)
        sent.append(copy)

    copies = []
    for slot, by in enumerate((4, -4, 8)):
        spread(copies, bc_all.at[own_class + own_turn], slot, by)
    for copy in copies:
        copy.wait_recv()
    copies = []
    spread(copies, bc_all.at[pl.ds(own_class, 4)], 3, 1)
    spread(copies, bc_all.at[pl.ds(own_class, 4)], 4, -1)
    spread(copies, bc_all.at[own_class + own_turn], 5, 2)
    spread(copies, bc_all.at[own_class + turn(own_turn, 1, 4)], 6, 2)
    spread(copies, bc_all.at[own_class + turn(own_turn, 1, 4)], 7, -2)
    spread(copies, bc_all.at[own_class + turn(own_turn, 2, 4)], 8, -2)
    for copy in copies:
        copy.wait_recv()
    for k in LATE:
        move(k % NZ)

    def choose(section, j):
        return bc_all[reads_ref[4 * section + j]]

    choice_copies = []
    for k in range(1, NS):
        for j in range(4):
            chosen[k - 1, j] = choose(sections[k - 1], j)
        copy = send(
            chosen.at[k - 1], groups_in.at[s], c_send.at[k - 1], c_recv.at[k - 1],
            (sections[k - 1], t, d),
        )
        choice_copies.append(copy)
        sent.append(copy)
    for j in range(4):
        groups_in[s, j] = choose(s, j)
    give(rows_all.at[d], lambda i: rows_all.at[i], o_send, o_recv)

    for copy in part_copies + step_copies:
        copy.wait_recv()
    heads = [None] * NZ
    for i in range(NZ):
        value = parts[s, i].astype(F32)
        for k in range(NS - 1):
            value = value + parts_in[k, i].astype(F32)
        product[block_of(i), :, 0:128] = value
    raw = step_parts[s]
    for k in range(NS - 1):
        raw = raw + steps_in[k]

    raw = jnp.concatenate(
        [
            jnp.concatenate(
                [raw[2 * c + i // 2 : 2 * c + i // 2 + 1, 64 * (i % 2) + 32 * m : 64 * (i % 2) + 32 * m + 32]
                 for i in range(4)],
                axis=1,
            )
            for m in range(2)
            for c in range(4)
        ],
        axis=0,
    )
    raw = raw + scalars_ref[8 + s]
    step = jnp.maximum(raw, 0.0) + jnp.log1p(jnp.exp(-jnp.abs(raw)))
    log_decay = -step * jnp.exp(jnp.full((8, 128), scalars_ref[s], F32))
    skip = scalars_ref[16 + s]
    taps = head_taps_ref[s].astype(F32)
    taps = jnp.concatenate([taps, taps], axis=1)
    lane = lax.broadcasted_iota(jnp.int32, (128, 128), 1)
    row = lax.broadcasted_iota(jnp.int32, (128, 128), 0)
    causal = row >= lane
    upto = (row <= lane).astype(F32)
    same = (row == lane).astype(F32)
    exact = lax.Precision.HIGHEST
    cum = jnp.dot(log_decay, upto, precision=exact, preferred_element_type=F32)
    both = jnp.concatenate([cum, step], axis=0)
    columns = lax.dot_general(same, both, dims(1, 1), precision=exact, preferred_element_type=F32)
    tall = lax.broadcasted_iota(jnp.int32, (512, 128), 0)
    for copy in choice_copies:
        copy.wait_recv()
    gated = []
    for m in range(2):
        v = product[:, 32 * m : 32 * m + 32, 0:128].reshape(512, 128)
        u = taps[3:4, :] * v
        for back in range(1, KERNEL):
            moved = jnp.where(tall >= back, pltpu.roll(v, back, 0), 0.0)
            u = u + taps[3 - back : 4 - back, :] * moved
        x = (u / (1.0 + jnp.exp(-u))).astype(BF16)
        state = jnp.zeros((STATE, 128), F32)
        outs = []
        for c in range(4):
            at = 4 * m + c

            def pick(j):
                part = groups_in[2 * c : 2 * c + 2, j].reshape(2, 2, 2, 32, 128)
                return part[:, :, m].reshape(128, 128)

            b = jnp.concatenate([pick(0), pick(1)], axis=1)
            cc = jnp.concatenate([pick(2), pick(3)], axis=1)
            xc = x[128 * c : 128 * c + 128]
            xf = xc.astype(F32)
            cum_c, step_c = columns[:, at : at + 1], columns[:, 8 + at : 9 + at]
            cum_r, step_r = cum[at : at + 1, :], step[at : at + 1, :]
            scores = lax.dot_general(cc, b, dims(1, 1), preferred_element_type=F32)
            mixing = jnp.exp(jnp.where(causal, cum_c - cum_r, -1e30)) * step_r
            y = jnp.dot((scores * mixing).astype(BF16), xc, preferred_element_type=F32)
            y = y + jnp.exp(cum_c) * jnp.dot(cc, state.astype(BF16), preferred_element_type=F32)
            y = y + skip * xf
            outs.append(y)
            if c < 3:
                end = cum[at : at + 1, 127:128]
                tail = (jnp.exp(end - cum_c) * step_c * xf).astype(BF16)
                state = jnp.exp(end) * state + lax.dot_general(
                    b, tail, dims(0, 0), preferred_element_type=F32
                )
        z = pltpu.roll(v, 64, 1)
        gated.append(jnp.concatenate(outs, axis=0) * (z / (1.0 + jnp.exp(-z))))
    wide = lax.broadcasted_iota(jnp.int32, (512, 128), 1)
    packed = jnp.where(wide < 64, gated[0], pltpu.roll(gated[1], 64, 1))
    own_gated[...] = packed.astype(BF16)

    y = lax.rem(s, 4)
    own_hot = hot_ref[:, pl.ds(pl.multiple_of(128 * s, 128), 128)]
    for j in range(4):
        part = packed[128 * j : 128 * j + 128]
        own_squares[j] = lax.dot_general(
            own_hot, (part * part).astype(BF16), dims(1, 1), preferred_element_type=F32
        )[:8]
    square_copies = []
    for k in range(1, NS):
        copy = send(
            own_squares.at[lax.rem(sections[k - 1], 4)], squares_in.at[k - 1],
            u_send.at[k - 1], u_recv.at[k - 1], (sections[k - 1], t, d),
        )
        square_copies.append(copy)
        sent.append(copy)
    gather_copies = []
    for k in range(1, NS):
        copy = send(
            own_gated, gathered.at[s], g_send.at[k - 1], g_recv.at[k - 1], (sections[k - 1], t, d)
        )
        gather_copies.append(copy)
        sent.append(copy)
    gathered[s] = own_gated[...]
    for copy in square_copies:
        copy.wait_recv()
    value = own_squares[y]
    for k in range(NS - 1):
        value = value + squares_in[k]
    squares[...] = value
    copies = []
    for k in range(1, NZ):
        copy = send(
            squares, z_squares.at[k - 1], q_send.at[k - 1], q_recv.at[k - 1],
            (s, turn(t, k, NZ), d),
        )
        copies.append(copy)
        sent.append(copy)
    for copy in copies:
        copy.wait_recv()
    for k in range(NZ - 1):
        value = value + z_squares[k]
    totals[y] = value
    copies = []
    for k in range(1, 4):
        copy = send(
            totals.at[y], totals.at[y], y_send.at[k - 1], y_recv.at[k - 1],
            (s - y + turn(y, k, 4), t, d),
        )
        copies.append(copy)
        sent.append(copy)
    forward_weights(2)
    for copy in copies + gather_copies:
        copy.wait_recv()
    have_weights(2)

    wide = lax.broadcasted_iota(jnp.int32, (128, 128), 1)
    gain = gain_ref[...].astype(F32)
    gain = jnp.concatenate([gain, gain], axis=1)
    for j in range(4):
        inverse = lax.rsqrt(totals[j] / (GROUP_HEADS * 64) + 1e-05)
        high = inverse.astype(BF16)
        low = (inverse - high.astype(F32)).astype(BF16)
        scale = lax.dot_general(
            jnp.concatenate([high, low], axis=0), hot_ref[...], dims(0, 0),
            preferred_element_type=F32,
        )
        first, second = [], []
        for i in range(0, NS, 2):
            pair = []
            for h in (i, i + 1):
                span = slice(128 * h, 128 * h + 128)
                value = gathered[h, 128 * j : 128 * j + 128, :].astype(F32)
                pair.append(value * scale[:, span] * gain[h : h + 1, :])
            even, odd = pair
            first.append(jnp.where(wide < 64, even, pltpu.roll(odd, 64, 1)).astype(BF16))
            second.append(jnp.where(wide < 64, pltpu.roll(even, 64, 1), odd).astype(BF16))
        lhs = jnp.concatenate(
            [jnp.concatenate(first, axis=1), jnp.concatenate(second, axis=1)], axis=0
        )
        for i in range(ND):
            result = jnp.dot(lhs, rows_all[i], preferred_element_type=F32)
            for m in range(2):
                product[
                    4 * j : 4 * j + 4, 32 * m : 32 * m + 32, 256 * i : 256 * i + 256
                ] = result[128 * m : 128 * m + 128].reshape(4, 32, 256)

    from_left, from_right = [None] * CHUNKS, [None] * CHUNKS
    for step in range(8):
        for h in range(CHUNKS):
            span = slice(WIDTH * h, WIDTH * h + WIDTH)
            value = product[turn(t, 8 - step, NZ), :, span]
            if step > 0:
                from_left[h].wait_recv()
                value = value + right_in[step - 1, h].astype(F32)
            right_out[step, h] = value.astype(BF16)
            from_left[h] = send(
                right_out.at[step, h], right_in.at[step, h],
                sr_send.at[step, h], sr_recv.at[step, h], right,
            )
            sent.append(from_left[h])
            if step < 7:
                value = product[turn(t, step - 7, NZ), :, span]
                if step > 0:
                    from_right[h].wait_recv()
                    value = value + left_in[step - 1, h].astype(F32)
                left_out[step, h] = value.astype(BF16)
                from_right[h] = send(
                    left_out.at[step, h], left_in.at[step, h],
                    sl_send.at[step, h], sl_recv.at[step, h], left,
                )
                sent.append(from_right[h])
    for h in range(CHUNKS):
        span = slice(WIDTH * h, WIDTH * h + WIDTH)
        from_left[h].wait_recv()
        from_right[h].wait_recv()
        value = product[t, :, span] + act_ref[:, span].astype(F32)
        value = value + right_in[7, h].astype(F32) + left_in[6, h].astype(F32)
        mixed_out[t, :, span] = value.astype(BF16)

    rings = [[None, None] for _ in range(CHUNKS)]
    for step in range(9):
        for c in range(CHUNKS):
            rows = pl.ds(ROWS * c, ROWS)
            if step > 0:
                rings[c][0].wait_recv()
            if step < 8:
                block = turn(t, -step, NZ)
                rings[c][0] = send(
                    mixed_out.at[block, rows], mixed_out.at[block, rows],
                    gr_send.at[step, c], gr_recv.at[step, c], right,
                )
                sent.append(rings[c][0])
            if 0 < step < 8:
                rings[c][1].wait_recv()
            if step < 7:
                block = turn(t, step, NZ)
                rings[c][1] = send(
                    mixed_out.at[block, rows], mixed_out.at[block, rows],
                    gl_send.at[step, c], gl_recv.at[step, c], left,
                )
                sent.append(rings[c][1])
        if step == 0:
            for copy in moves:
                copy.wait_recv()
            for k in range(NS):
                new_xz[:, 128 * k : 128 * k + 128] = xz_coming[origin_ref[k]]
                new_rows[64 * k : 64 * k + 64, :] = rows_coming[origin_ref[k]]
    for copy in sent:
        copy.wait_send()


def layer_call(*operands):
    def dma(*shape):
        return [pltpu.SemaphoreType.DMA(shape)] * 2

    return pl.pallas_call(
        layer_kernel,
        out_shape=(
            jax.ShapeDtypeStruct((NZ, 64, 1024), BF16),
            jax.ShapeDtypeStruct((256, 1024), BF16),
            jax.ShapeDtypeStruct((512, 256), BF16),
        ),
        in_specs=[SMEM] * 5 + [VMEM] * 8,
        out_specs=(VMEM,) * 3,
        scratch_shapes=[
            pltpu.VMEM((16, 1024), BF16),
            pltpu.VMEM((NZ, 64, 1024), BF16),
            pltpu.VMEM((1024, 1024), BF16),
            pltpu.VMEM((ND, 16, 256), BF16),
            pltpu.VMEM((ND, 512, 256), BF16),
            pltpu.VMEM((NS, NZ, 64, 128), BF16),
            pltpu.VMEM((NS - 1, NZ, 64, 128), BF16),
            pltpu.VMEM((NZ + 1, 64, 128), BF16),
            pltpu.VMEM((NS - 1, 3, 64, 128), BF16),
            pltpu.VMEM((NS, 8, 128), F32),
            pltpu.VMEM((NS - 1, 8, 128), F32),
            pltpu.VMEM((NZ, 128, 128), BF16),
            pltpu.VMEM((NS - 1, 4, 128, 128), BF16),
            pltpu.VMEM((NS, 4, 128, 128), BF16),
            pltpu.VMEM((NZ - 1, 256, 128), BF16),
            pltpu.VMEM((NZ, 256, 128), BF16),
            pltpu.VMEM((NZ - 1, 64, 256), BF16),
            pltpu.VMEM((NZ, 64, 256), BF16),
            pltpu.VMEM((512, 128), BF16),
            pltpu.VMEM((NS, 512, 128), BF16),
            pltpu.VMEM((4, 8, 128), F32),
            pltpu.VMEM((NS - 1, 8, 128), F32),
            pltpu.VMEM((8, 128), F32),
            pltpu.VMEM((NZ - 1, 8, 128), F32),
            pltpu.VMEM((4, 8, 128), F32),
            pltpu.VMEM((NZ, 64, 1024), F32),
            pltpu.VMEM((8, CHUNKS, 64, WIDTH), BF16),
            pltpu.VMEM((8, CHUNKS, 64, WIDTH), BF16),
            pltpu.VMEM((7, CHUNKS, 64, WIDTH), BF16),
            pltpu.VMEM((7, CHUNKS, 64, WIDTH), BF16),
            *dma(3), *dma(3), *dma(3),
            *dma(8, CHUNKS), *dma(7, CHUNKS),
            *dma(NS - 1, 4), *dma(NS - 1), *dma(NS - 1),
            *dma(9), *dma(NS - 1), *dma(NZ - 1), *dma(NZ - 1),
            *dma(NS - 1), *dma(NZ - 1), *dma(NS - 1), *dma(3),
            *dma(8, CHUNKS), *dma(7, CHUNKS), *dma(8, CHUNKS), *dma(7, CHUNKS),
        ],
        compiler_params=pltpu.CompilerParams(
            collective_id=0, has_side_effects=True, vmem_limit_bytes=36 << 20
        ),
        cost_estimate=pl.CostEstimate(
            flops=4_000_000_000, bytes_accessed=100_000_000, transcendentals=0
        ),
    )(*operands)


def head_maps(old_heads, new_heads, member):
    both = jnp.stack([old_heads, new_heads]).reshape(2, NZ, NS)
    mine = lax.dynamic_index_in_dim(both, member, 1, keepdims=False)
    groups = mine[0] // GROUP_HEADS
    j = jnp.arange(4, dtype=jnp.int32)
    block = 8 * (j // 2) + 2 * groups[:, None] + j % 2
    reads = (4 * (block % 4) + block // 4).reshape(4 * NS)
    slots = jnp.arange(NS, dtype=jnp.int32)
    devices = jnp.arange(NZ, dtype=jnp.int32)
    leaving = jnp.sum(
        jnp.where(both[1][:, :, None] == mine[0], slots, 0), axis=(1, 2), dtype=jnp.int32
    )
    origin = jnp.sum(
        jnp.where(both[0][:, :, None] == mine[1], devices[:, None, None], 0),
        axis=(0, 1),
        dtype=jnp.int32,
    )
    return groups, reads, leaving, origin


def per_device(
    activations,
    old_heads,
    new_heads,
    xz_weight,
    dt_weight,
    bc_weight,
    conv_heads,
    conv_groups,
    decay_log,
    dt_bias,
    skip_gain,
    norm_gain,
    out_weight,
):
    _, t, _ = place()
    groups, reads, leaving, origin = head_maps(old_heads, new_heads, t)
    mixed, new_xz, new_out = layer_call(
        groups,
        reads,
        leaving,
        origin,
        jnp.concatenate([decay_log, dt_bias, skip_gain]).astype(F32),
        jnp.transpose(activations, (1, 0, 2)).reshape(64, 1024),
        jnp.transpose(xz_weight, (1, 0, 2)),
        jnp.pad(jnp.transpose(dt_weight), ((0, 8), (0, 0))),
        bc_weight,
        out_weight,
        conv_groups,
        conv_heads,
        norm_gain,
    )
    mixed = jnp.transpose(mixed.reshape(16, 2, 32, 1024), (0, 2, 1, 3)).reshape(512, 2, 1024)
    return mixed, new_xz.reshape(256, 8, 128), new_out.reshape(8, 64, 256)


def solution(mesh):
    in_specs = (
        P("tensor", "dp", "section"),
        P(),
        P(),
        P(("section", "dp"), "tensor", None),
        P(("section", "dp"), "tensor"),
        P("section", "tensor"),
        P("tensor", None, None),
        P(None, "tensor"),
        P("tensor"),
        P("tensor"),
        P("tensor"),
        P("tensor", None),
        P("tensor", None, ("section", "dp")),
    )
    out_specs = (
        P(None, "dp", "section"),
        P(("section", "dp"), "tensor", None),
        P("tensor", None, ("section", "dp")),
    )
    return jax.shard_map(
        per_device, mesh=mesh, in_specs=in_specs, out_specs=out_specs, check_vma=False
    )
```

```python
import jax
import jax.numpy as jnp
from jax import lax
from jax.experimental import pallas as pl
from jax.experimental.pallas import tpu as pltpu
from jax.sharding import PartitionSpec as P

STATE = 256
GROUP_HEADS = 32
KERNEL = 4
MESH = pl.DeviceIdType.MESH
NZ, NS, ND = 16, 8, 4
CHUNKS = 4
WIDTH = 1024 // CHUNKS
WHOLE = ((8,), (1, -1, 2, -2, 3, -3), (7, -7, 6, -6, 5, -5))
PIECES = ((), (4, -4), ())
VMEM = pl.BlockSpec(memory_space=pltpu.VMEM)
SMEM = pl.BlockSpec(memory_space=pltpu.SMEM)
HBM = pl.BlockSpec(memory_space=pltpu.HBM)
F32, BF16 = jnp.float32, jnp.bfloat16
ARRIVAL = (0, -1, 1, -2, 2, -3, 3, -4, 4, -5, 5, -6, 6, -7, 7, -8)


def place():
    return lax.axis_index("section"), lax.axis_index("tensor"), lax.axis_index("dp")


def turn(index, by, size):
    return lax.rem(index + (by % size), size)


def greet(peers):
    barrier = pltpu.get_barrier_semaphore()
    for peer in peers:
        pl.semaphore_signal(barrier, inc=1, device_id=peer, device_id_type=MESH)
    pl.semaphore_wait(barrier, len(peers))


def send(source, target, send_sem, recv_sem, peer):
    copy = pltpu.make_async_remote_copy(
        src_ref=source,
        dst_ref=target,
        send_sem=send_sem,
        recv_sem=recv_sem,
        device_id=peer,
        device_id_type=MESH,
    )
    copy.start()
    return copy


def dims(lhs, rhs):
    return (((lhs,), (rhs,)), ((), ()))


def layer_kernel(
    groups_ref, reads_ref, leaving_ref, origin_ref, scalars_ref,
    act_ref, xz_ref, dt_ref, bc_hbm, out_hbm, group_taps_hbm, head_taps_hbm, gain_hbm,
    mixed_out, new_xz, new_rows,
    bc_ref, out_ref, group_taps_ref, head_taps_ref, gain_ref, load_sem,
    hot_ref, acts, weights, dts, rows_all, parts, parts_in, bc_parts, bc_in, step_parts, steps_in,
    bc_all, chosen, groups_in, xz_leaving, xz_coming, rows_leaving, rows_coming,
    own_gated, gathered, own_squares, squares_in, squares, z_squares, totals, product,
    right_out, right_in, left_out, left_in,
    w_send, w_recv, d_send, d_recv, o_send, o_recv, right_send, right_recv,
    left_send, left_recv, p_send, p_recv, b_send, b_recv, s_send, s_recv,
    z_send, z_recv, c_send, c_recv, e_send, e_recv, f_send, f_recv,
    g_send, g_recv, q_send, q_recv, u_send, u_recv, y_send, y_recv,
    sr_send, sr_recv, sl_send, sl_recv, gr_send, gr_recv, gl_send, gl_recv,
):
    s, t, d = place()
    right, left = (s, turn(t, 1, NZ), d), (s, turn(t, -1, NZ), d)
    sections = [turn(s, k, NS) for k in range(1, NS)]
    core = d + 1 - 2 * lax.rem(d, 2)
    across = turn(d, 2, ND)
    loads = [
        pltpu.make_async_copy(source, target, load_sem.at[i])
        for i, (source, target) in enumerate(
            (
                (out_hbm, out_ref),
                (bc_hbm, bc_ref),
                (group_taps_hbm, group_taps_ref),
                (head_taps_hbm, head_taps_ref),
                (gain_hbm, gain_ref),
            )
        )
    ]
    for load in loads:
        load.start()
    greet(
        [(s, turn(t, k, NZ), d) for k in range(1, NZ)]
        + [(p, t, d) for p in sections]
        + [(s, t, core), (s, t, across)]
    )
    sent = []

    def rows_at(index):
        return weights.at[pl.ds(pl.multiple_of(index * 256, 256), 256)]

    gathers = []

    def give(own, slot_of, ss, rs):
        near = send(own, slot_of(d), ss.at[0], rs.at[0], (s, t, core))
        far = send(own, slot_of(d), ss.at[1], rs.at[1], (s, t, across))
        sent.extend([near, far])
        gathers.append((slot_of, ss, rs, near, far))

    def start_ring(c):
        span = pl.ds(WIDTH * c, WIDTH)
        return [
            send(act_ref.at[:, span], acts.at[t, :, span], right_send.at[0, c], right_recv.at[0, c], right),
            send(act_ref.at[:, span], acts.at[t, :, span], left_send.at[0, c], left_recv.at[0, c], left),
        ]

    rings = [start_ring(c) for c in range(CHUNKS)]
    for ring in rings:
        sent.extend(ring)
    own_rows = pl.ds(pl.multiple_of(d * 256, 256), 256)
    for h in range(NS):
        weights[own_rows, 128 * h : 128 * h + 128] = xz_ref[h]
    give(rows_at(d), rows_at, w_send, w_recv)
    give(dt_ref, lambda i: dts.at[i], d_send, d_recv)
    acts[t] = act_ref[...]
    dts[d] = dt_ref[...]
    for load in loads:
        load.wait()
    rows_all[d] = out_ref[...].reshape(512, 256)
    lane = lax.broadcasted_iota(jnp.int32, (16, 128), 1)
    row = lax.rem(lax.broadcasted_iota(jnp.int32, (16, 128), 0), 8)
    halves = jnp.where(lane < 64, 0, 4)
    for h in range(NS):
        hot_ref[:, 128 * h : 128 * h + 128] = (row == halves + groups_ref[h]).astype(F32).astype(BF16)

    def pack(k):
        there = turn(t, k, NZ)
        if k == 0:
            xz_coming[t] = xz_ref[leaving_ref[there]]
            rows_coming[t] = out_ref[leaving_ref[there]]
        else:
            xz_leaving[k - 1] = xz_ref[leaving_ref[there]]
            rows_leaving[k - 1] = out_ref[leaving_ref[there]]

    for k in range(NZ):
        pack(k)
    moves = []

    def move(k, piece=None):
        there = (s, turn(t, k, NZ), d)
        parts_of = []
        if piece is None:
            parts_of.append((xz_leaving.at[k - 1], xz_coming.at[t], e_send.at[k - 1, 0], e_recv.at[k - 1, 0]))
            parts_of.append((rows_leaving.at[k - 1], rows_coming.at[t], f_send.at[k - 1, 0], f_recv.at[k - 1, 0]))
        elif piece < 4:
            rows = pl.ds(64 * piece, 64)
            parts_of.append(
                (xz_leaving.at[k - 1, rows], xz_coming.at[t, rows], e_send.at[k - 1, piece], e_recv.at[k - 1, piece])
            )
        else:
            half = piece - 4
            rows = pl.ds(32 * half, 32)
            parts_of.append(
                (rows_leaving.at[k - 1, rows], rows_coming.at[t, rows], f_send.at[k - 1, half], f_recv.at[k - 1, half])
            )
        for source, target, ss, rs in parts_of:
            copy = send(source, target, ss, rs, there)
            moves.append(copy)
            sent.append(copy)

    def move_whole(point):
        for k in WHOLE[point]:
            move(k % NZ)

    def move_pieces(ring, step):
        for k in PIECES[ring]:
            if step < 6:
                move(k % NZ, step)

    move_whole(0)
    forwarded = []

    def forward_weights(which):
        slot_of, ss, rs, near, far = gathers[which]
        far.wait_recv()
        copy = send(slot_of(across), slot_of(across), ss.at[2], rs.at[2], (s, t, core))
        forwarded.append(copy)
        sent.append(copy)

    def have_weights(which):
        gathers[which][3].wait_recv()
        forwarded[which].wait_recv()

    def block_of(i):
        return turn(t, ARRIVAL[i], NZ)

    part_copies = []

    def project(group):
        rows = jnp.concatenate([acts[block_of(4 * group + i)] for i in range(4)], axis=0)
        for half in range(2):
            result = jnp.dot(
                rows, weights[:, 512 * half : 512 * half + 512], preferred_element_type=F32
            ).astype(BF16)
            for j in range(4):
                parts[4 * half + j, 4 * group : 4 * group + 4] = result[
                    :, 128 * j : 128 * j + 128
                ].reshape(4, 64, 128)
        for k in range(1, NS):
            span = pl.ds(4 * group, 4)
            copy = send(
                parts.at[sections[k - 1], span],
                parts_in.at[k - 1, span],
                p_send.at[k - 1, group],
                p_recv.at[k - 1, group],
                (sections[k - 1], t, d),
            )
            part_copies.append(copy)
            sent.append(copy)

    for step in range(1, 9):
        for c in range(CHUNKS):
            span = pl.ds(WIDTH * c, WIDTH)
            rings[c][0].wait_recv()
            if step < 8:
                block = turn(t, -step, NZ)
                copy = send(
                    acts.at[block, :, span], acts.at[block, :, span],
                    right_send.at[step, c], right_recv.at[step, c], right,
                )
                rings[c][0] = copy
                sent.append(copy)
            if step < 8:
                rings[c][1].wait_recv()
            if step < 7:
                block = turn(t, step, NZ)
                copy = send(
                    acts.at[block, :, span], acts.at[block, :, span],
                    left_send.at[step, c], left_recv.at[step, c], left,
                )
                rings[c][1] = copy
                sent.append(copy)
        move_pieces(0, step - 1)
        if step == 3:
            forward_weights(0)
            forward_weights(1)
        if step == 4:
            have_weights(0)
            have_weights(1)
            project(0)
        if step == 5:
            project(1)

    bc_parts[0] = jnp.zeros((64, 128), BF16)
    for i in range(4):
        result = jnp.dot(
            acts[4 * i : 4 * i + 4].reshape(256, 1024), bc_ref[...], preferred_element_type=F32
        )
        bc_parts[1 + 4 * i : 5 + 4 * i] = result.astype(BF16).reshape(4, 64, 128)
    bc_copies = []
    for k in range(1, NS):
        copy = send(
            bc_parts.at[pl.ds(2 * sections[k - 1], 3)],
            bc_in.at[k - 1],
            b_send.at[k - 1],
            b_recv.at[k - 1],
            (sections[k - 1], t, d),
        )
        bc_copies.append(copy)
        sent.append(copy)
    move_whole(1)
    project(2)
    project(3)
    raw = jnp.zeros((16, 1024), F32)
    for i in range(ND):
        raw = raw + lax.dot_general(
            dts[i],
            acts[:, :, 256 * i : 256 * i + 256].reshape(1024, 256),
            dims(1, 1),
            preferred_element_type=F32,
        )
    for j in range(NS):
        for r in range(8):
            step_parts[j, r : r + 1, :] = raw[j : j + 1, 128 * r : 128 * r + 128]
    step_copies = []
    for k in range(1, NS):
        copy = send(
            step_parts.at[sections[k - 1]],
            steps_in.at[k - 1],
            s_send.at[k - 1],
            s_recv.at[k - 1],
            (sections[k - 1], t, d),
        )
        step_copies.append(copy)
        sent.append(copy)

    for copy in bc_copies:
        copy.wait_recv()
    total = bc_parts[pl.ds(2 * s, 3)].astype(F32)
    for k in range(NS - 1):
        total = total + bc_in[k].astype(F32)
    own_class, own_turn = 4 * lax.rem(t, 4), t // 4
    taps = group_taps_ref[...].astype(F32)
    for m in range(2):
        rows = total[:, 32 * m : 32 * m + 32, :].reshape(96, 128)
        u = jnp.zeros((64, 128), F32)
        for k in range(KERNEL):
            u = u + taps[k : k + 1, :] * rows[29 + k : 93 + k]
        u = (u / (1.0 + jnp.exp(-u))).astype(BF16)
        bc_all[own_class + own_turn, 32 * m : 32 * m + 32, :] = u[:32]
        bc_all[own_class + own_turn, 64 + 32 * m : 96 + 32 * m, :] = u[32:]

    def spread(copies, source, slot, by):
        copy = send(source, source, z_send.at[slot], z_recv.at[slot], (s, turn(t, by, NZ), d))
        copies.append(copy)
        sent.append(copy)

    def gather_parts(start, stop):
        for i in range(start, stop):
            value = parts[s, i].astype(F32)
            for k in range(NS - 1):
                value = value + parts_in[k, i].astype(F32)
            product[block_of(i), :, 0:128] = value

    copies = []
    for slot, by in enumerate((4, -4, 8)):
        spread(copies, bc_all.at[own_class + own_turn], slot, by)
    for copy in part_copies[: 2 * NS - 2]:
        copy.wait_recv()
    gather_parts(0, 8)
    for copy in copies:
        copy.wait_recv()
    copies = []
    spread(copies, bc_all.at[pl.ds(own_class, 4)], 3, 1)
    spread(copies, bc_all.at[pl.ds(own_class, 4)], 4, -1)
    spread(copies, bc_all.at[own_class + own_turn], 5, 2)
    spread(copies, bc_all.at[own_class + turn(own_turn, 1, 4)], 6, 2)
    spread(copies, bc_all.at[own_class + turn(own_turn, 1, 4)], 7, -2)
    spread(copies, bc_all.at[own_class + turn(own_turn, 2, 4)], 8, -2)
    for copy in copies:
        copy.wait_recv()
    move_whole(2)

    def choose(section, j):
        return bc_all[reads_ref[4 * section + j]]

    choice_copies = []
    for k in range(1, NS):
        for j in range(4):
            chosen[k - 1, j] = choose(sections[k - 1], j)
        copy = send(
            chosen.at[k - 1], groups_in.at[s], c_send.at[k - 1], c_recv.at[k - 1],
            (sections[k - 1], t, d),
        )
        choice_copies.append(copy)
        sent.append(copy)
    for j in range(4):
        groups_in[s, j] = choose(s, j)
    give(rows_all.at[d], lambda i: rows_all.at[i], o_send, o_recv)

    for copy in part_copies[2 * NS - 2 :] + step_copies:
        copy.wait_recv()
    gather_parts(8, NZ)
    raw = step_parts[s]
    for k in range(NS - 1):
        raw = raw + steps_in[k]

    raw = jnp.concatenate(
        [
            jnp.concatenate(
                [raw[2 * c + i // 2 : 2 * c + i // 2 + 1, 64 * (i % 2) + 32 * m : 64 * (i % 2) + 32 * m + 32]
                 for i in range(4)],
                axis=1,
            )
            for m in range(2)
            for c in range(4)
        ],
        axis=0,
    )
    raw = raw + scalars_ref[8 + s]
    step = jnp.maximum(raw, 0.0) + jnp.log1p(jnp.exp(-jnp.abs(raw)))
    log_decay = -step * jnp.exp(jnp.full((8, 128), scalars_ref[s], F32))
    skip = scalars_ref[16 + s]
    taps = head_taps_ref[s].astype(F32)
    taps = jnp.concatenate([taps, taps], axis=1)
    lane = lax.broadcasted_iota(jnp.int32, (128, 128), 1)
    row = lax.broadcasted_iota(jnp.int32, (128, 128), 0)
    causal = row >= lane
    upto = (row <= lane).astype(F32)
    same = (row == lane).astype(F32)
    exact = lax.Precision.HIGHEST
    cum = jnp.dot(log_decay, upto, precision=exact, preferred_element_type=F32)
    both = jnp.concatenate([cum, step], axis=0)
    columns = lax.dot_general(same, both, dims(1, 1), precision=exact, preferred_element_type=F32)
    tall = lax.broadcasted_iota(jnp.int32, (512, 128), 0)
    for copy in choice_copies:
        copy.wait_recv()
    gated = []
    for m in range(2):
        v = product[:, 32 * m : 32 * m + 32, 0:128].reshape(512, 128)
        u = taps[3:4, :] * v
        for back in range(1, KERNEL):
            moved = jnp.where(tall >= back, pltpu.roll(v, back, 0), 0.0)
            u = u + taps[3 - back : 4 - back, :] * moved
        x = (u / (1.0 + jnp.exp(-u))).astype(BF16)
        state = jnp.zeros((STATE, 128), F32)
        outs = []
        for c in range(4):
            at = 4 * m + c

            def pick(j):
                part = groups_in[2 * c : 2 * c + 2, j].reshape(2, 2, 2, 32, 128)
                return part[:, :, m].reshape(128, 128)

            b = jnp.concatenate([pick(0), pick(1)], axis=1)
            cc = jnp.concatenate([pick(2), pick(3)], axis=1)
            xc = x[128 * c : 128 * c + 128]
            xf = xc.astype(F32)
            cum_c, step_c = columns[:, at : at + 1], columns[:, 8 + at : 9 + at]
            cum_r, step_r = cum[at : at + 1, :], step[at : at + 1, :]
            scores = lax.dot_general(cc, b, dims(1, 1), preferred_element_type=F32)
            mixing = jnp.exp(jnp.where(causal, cum_c - cum_r, -1e30)) * step_r
            y = jnp.dot((scores * mixing).astype(BF16), xc, preferred_element_type=F32)
            y = y + jnp.exp(cum_c) * jnp.dot(cc, state.astype(BF16), preferred_element_type=F32)
            y = y + skip * xf
            outs.append(y)
            if c < 3:
                end = cum[at : at + 1, 127:128]
                tail = (jnp.exp(end - cum_c) * step_c * xf).astype(BF16)
                state = jnp.exp(end) * state + lax.dot_general(
                    b, tail, dims(0, 0), preferred_element_type=F32
                )
        z = pltpu.roll(v, 64, 1)
        gated.append(jnp.concatenate(outs, axis=0) * (z / (1.0 + jnp.exp(-z))))
    wide = lax.broadcasted_iota(jnp.int32, (512, 128), 1)
    packed = jnp.where(wide < 64, gated[0], pltpu.roll(gated[1], 64, 1))
    own_gated[...] = packed.astype(BF16)

    y = lax.rem(s, 4)
    own_hot = hot_ref[:, pl.ds(pl.multiple_of(128 * s, 128), 128)]
    for j in range(4):
        part = packed[128 * j : 128 * j + 128]
        own_squares[j] = lax.dot_general(
            own_hot, (part * part).astype(BF16), dims(1, 1), preferred_element_type=F32
        )[:8]
    square_copies = []
    for k in range(1, NS):
        copy = send(
            own_squares.at[lax.rem(sections[k - 1], 4)], squares_in.at[k - 1],
            u_send.at[k - 1], u_recv.at[k - 1], (sections[k - 1], t, d),
        )
        square_copies.append(copy)
        sent.append(copy)
    gather_copies = []
    for k in range(1, NS):
        copy = send(
            own_gated, gathered.at[s], g_send.at[k - 1], g_recv.at[k - 1], (sections[k - 1], t, d)
        )
        gather_copies.append(copy)
        sent.append(copy)
    gathered[s] = own_gated[...]
    for copy in square_copies:
        copy.wait_recv()
    value = own_squares[y]
    for k in range(NS - 1):
        value = value + squares_in[k]
    squares[...] = value
    copies = []
    for k in range(1, NZ):
        copy = send(
            squares, z_squares.at[k - 1], q_send.at[k - 1], q_recv.at[k - 1],
            (s, turn(t, k, NZ), d),
        )
        copies.append(copy)
        sent.append(copy)
    for copy in copies:
        copy.wait_recv()
    for k in range(NZ - 1):
        value = value + z_squares[k]
    totals[y] = value
    copies = []
    for k in range(1, 4):
        copy = send(
            totals.at[y], totals.at[y], y_send.at[k - 1], y_recv.at[k - 1],
            (s - y + turn(y, k, 4), t, d),
        )
        copies.append(copy)
        sent.append(copy)
    forward_weights(2)
    for copy in copies + gather_copies:
        copy.wait_recv()
    have_weights(2)

    wide = lax.broadcasted_iota(jnp.int32, (128, 128), 1)
    gain = gain_ref[...].astype(F32)
    gain = jnp.concatenate([gain, gain], axis=1)

    def multiply(tile):
        inverse = lax.rsqrt(totals[tile] / (GROUP_HEADS * 64) + 1e-05)
        high = inverse.astype(BF16)
        low = (inverse - high.astype(F32)).astype(BF16)
        scale = lax.dot_general(
            jnp.concatenate([high, low], axis=0), hot_ref[...], dims(0, 0),
            preferred_element_type=F32,
        )
        first, second = [], []
        for i in range(0, NS, 2):
            pair = []
            for h in (i, i + 1):
                span = slice(128 * h, 128 * h + 128)
                value = gathered[h, pl.ds(pl.multiple_of(128 * tile, 128), 128), :].astype(F32)
                pair.append(value * scale[:, span] * gain[h : h + 1, :])
            even, odd = pair
            first.append(jnp.where(wide < 64, even, pltpu.roll(odd, 64, 1)).astype(BF16))
            second.append(jnp.where(wide < 64, pltpu.roll(even, 64, 1), odd).astype(BF16))
        lhs = jnp.concatenate(
            [jnp.concatenate(first, axis=1), jnp.concatenate(second, axis=1)], axis=0
        )
        for i in range(ND):
            result = jnp.dot(lhs, rows_all[i], preferred_element_type=F32)
            for m in range(2):
                product[
                    pl.ds(4 * tile, 4), 32 * m : 32 * m + 32, 256 * i : 256 * i + 256
                ] = result[128 * m : 128 * m + 128].reshape(4, 32, 256)

    first_tile = turn(t, 8, NZ) // 4
    for i in range(2):
        multiply(turn(first_tile, i, 4))

    from_left, from_right = [None] * CHUNKS, [None] * CHUNKS
    for step in range(8):
        if step == 1:
            for i in range(2, 4):
                multiply(turn(first_tile, i, 4))
        for h in range(CHUNKS):
            span = slice(WIDTH * h, WIDTH * h + WIDTH)
            value = product[turn(t, 8 - step, NZ), :, span]
            if step > 0:
                from_left[h].wait_recv()
                value = value + right_in[step - 1, h].astype(F32)
            right_out[step, h] = value.astype(BF16)
            from_left[h] = send(
                right_out.at[step, h], right_in.at[step, h],
                sr_send.at[step, h], sr_recv.at[step, h], right,
            )
            sent.append(from_left[h])
            if step < 7:
                value = product[turn(t, step - 7, NZ), :, span]
                if step > 0:
                    from_right[h].wait_recv()
                    value = value + left_in[step - 1, h].astype(F32)
                left_out[step, h] = value.astype(BF16)
                from_right[h] = send(
                    left_out.at[step, h], left_in.at[step, h],
                    sl_send.at[step, h], sl_recv.at[step, h], left,
                )
                sent.append(from_right[h])
        move_pieces(1, step)
    rings = []
    for h in range(CHUNKS):
        span = slice(WIDTH * h, WIDTH * h + WIDTH)
        from_left[h].wait_recv()
        from_right[h].wait_recv()
        value = product[t, :, span] + act_ref[:, span].astype(F32)
        value = value + right_in[7, h].astype(F32) + left_in[6, h].astype(F32)
        mixed_out[t, :, span] = value.astype(BF16)
        span = pl.ds(WIDTH * h, WIDTH)
        ring = []
        for ss, rs, peer in ((gr_send, gr_recv, right), (gl_send, gl_recv, left)):
            ring.append(
                send(mixed_out.at[t, :, span], mixed_out.at[t, :, span], ss.at[0, h], rs.at[0, h], peer)
            )
        sent.extend(ring)
        rings.append(ring)

    move_pieces(2, 0)
    for step in range(1, 9):
        for c in range(CHUNKS):
            span = pl.ds(WIDTH * c, WIDTH)
            rings[c][0].wait_recv()
            if step < 8:
                block = turn(t, -step, NZ)
                rings[c][0] = send(
                    mixed_out.at[block, :, span], mixed_out.at[block, :, span],
                    gr_send.at[step, c], gr_recv.at[step, c], right,
                )
                sent.append(rings[c][0])
            if step < 8:
                rings[c][1].wait_recv()
            if step < 7:
                block = turn(t, step, NZ)
                rings[c][1] = send(
                    mixed_out.at[block, :, span], mixed_out.at[block, :, span],
                    gl_send.at[step, c], gl_recv.at[step, c], left,
                )
                sent.append(rings[c][1])
        move_pieces(2, step)
        if step == 7:
            for copy in moves:
                copy.wait_recv()
            for k in range(NS):
                new_xz[:, 128 * k : 128 * k + 128] = xz_coming[origin_ref[k]]
                new_rows[64 * k : 64 * k + 64, :] = rows_coming[origin_ref[k]]
    for copy in sent:
        copy.wait_send()


def layer_call(*operands):
    def dma(*shape):
        return [pltpu.SemaphoreType.DMA(shape)] * 2

    return pl.pallas_call(
        layer_kernel,
        out_shape=(
            jax.ShapeDtypeStruct((NZ, 64, 1024), BF16),
            jax.ShapeDtypeStruct((256, 1024), BF16),
            jax.ShapeDtypeStruct((512, 256), BF16),
        ),
        in_specs=[SMEM] * 5 + [VMEM] * 3 + [HBM] * 5,
        out_specs=(VMEM,) * 3,
        scratch_shapes=[
            pltpu.VMEM((1024, 128), BF16),
            pltpu.VMEM((NS, 64, 256), BF16),
            pltpu.VMEM((KERNEL, 128), BF16),
            pltpu.VMEM((NS, KERNEL, 64), BF16),
            pltpu.VMEM((NS, 64), BF16),
            pltpu.SemaphoreType.DMA((5,)),
            pltpu.VMEM((16, 1024), BF16),
            pltpu.VMEM((NZ, 64, 1024), BF16),
            pltpu.VMEM((1024, 1024), BF16),
            pltpu.VMEM((ND, 16, 256), BF16),
            pltpu.VMEM((ND, 512, 256), BF16),
            pltpu.VMEM((NS, NZ, 64, 128), BF16),
            pltpu.VMEM((NS - 1, NZ, 64, 128), BF16),
            pltpu.VMEM((NZ + 1, 64, 128), BF16),
            pltpu.VMEM((NS - 1, 3, 64, 128), BF16),
            pltpu.VMEM((NS, 8, 128), F32),
            pltpu.VMEM((NS - 1, 8, 128), F32),
            pltpu.VMEM((NZ, 128, 128), BF16),
            pltpu.VMEM((NS - 1, 4, 128, 128), BF16),
            pltpu.VMEM((NS, 4, 128, 128), BF16),
            pltpu.VMEM((NZ - 1, 256, 128), BF16),
            pltpu.VMEM((NZ, 256, 128), BF16),
            pltpu.VMEM((NZ - 1, 64, 256), BF16),
            pltpu.VMEM((NZ, 64, 256), BF16),
            pltpu.VMEM((512, 128), BF16),
            pltpu.VMEM((NS, 512, 128), BF16),
            pltpu.VMEM((4, 8, 128), F32),
            pltpu.VMEM((NS - 1, 8, 128), F32),
            pltpu.VMEM((8, 128), F32),
            pltpu.VMEM((NZ - 1, 8, 128), F32),
            pltpu.VMEM((4, 8, 128), F32),
            pltpu.VMEM((NZ, 64, 1024), F32),
            pltpu.VMEM((8, CHUNKS, 64, WIDTH), BF16),
            pltpu.VMEM((8, CHUNKS, 64, WIDTH), BF16),
            pltpu.VMEM((7, CHUNKS, 64, WIDTH), BF16),
            pltpu.VMEM((7, CHUNKS, 64, WIDTH), BF16),
            *dma(3), *dma(3), *dma(3),
            *dma(8, CHUNKS), *dma(7, CHUNKS),
            *dma(NS - 1, 4), *dma(NS - 1), *dma(NS - 1),
            *dma(9), *dma(NS - 1), *dma(NZ - 1, 4), *dma(NZ - 1, 2),
            *dma(NS - 1), *dma(NZ - 1), *dma(NS - 1), *dma(3),
            *dma(8, CHUNKS), *dma(7, CHUNKS), *dma(8, CHUNKS), *dma(7, CHUNKS),
        ],
        compiler_params=pltpu.CompilerParams(
            collective_id=0, has_side_effects=True, vmem_limit_bytes=36 << 20
        ),
        cost_estimate=pl.CostEstimate(
            flops=4_000_000_000, bytes_accessed=100_000_000, transcendentals=0
        ),
    )(*operands)


def head_maps(old_heads, new_heads, member):
    both = lax.optimization_barrier(jnp.stack([old_heads, new_heads]))
    mine = lax.dynamic_slice_in_dim(both, member * NS, NS, 1)
    groups = mine[0] // GROUP_HEADS
    j = jnp.arange(4, dtype=jnp.int32)
    block = 8 * (j // 2) + 2 * groups[:, None] + j % 2
    reads = (4 * (block % 4) + block // 4).reshape(4 * NS)
    slots = jnp.arange(NS, dtype=jnp.int32)
    owner = jnp.arange(NZ * NS, dtype=jnp.int32) // NS
    there = owner == jnp.arange(NZ, dtype=jnp.int32)[:, None]
    moved = both[1][:, None] == mine[0]
    leaving = jnp.sum(
        jnp.where(there[:, :, None] & moved, slots, 0), axis=(1, 2), dtype=jnp.int32
    )
    origin = jnp.sum(
        jnp.where(both[0] == mine[1][:, None], owner, 0), axis=1, dtype=jnp.int32
    )
    return groups, reads, leaving, origin


def per_device(
    activations,
    old_heads,
    new_heads,
    xz_weight,
    dt_weight,
    bc_weight,
    conv_heads,
    conv_groups,
    decay_log,
    dt_bias,
    skip_gain,
    norm_gain,
    out_weight,
):
    _, t, _ = place()
    groups, reads, leaving, origin = head_maps(old_heads, new_heads, t)
    mixed, new_xz, new_out = layer_call(
        groups,
        reads,
        leaving,
        origin,
        jnp.concatenate([decay_log, dt_bias, skip_gain]).astype(F32),
        jnp.transpose(activations, (1, 0, 2)).reshape(64, 1024),
        jnp.transpose(xz_weight, (1, 0, 2)),
        jnp.pad(jnp.transpose(dt_weight), ((0, 8), (0, 0))),
        bc_weight,
        out_weight,
        conv_groups,
        conv_heads,
        norm_gain,
    )
    mixed = jnp.transpose(mixed.reshape(16, 2, 32, 1024), (0, 2, 1, 3)).reshape(512, 2, 1024)
    return mixed, new_xz.reshape(256, 8, 128), new_out.reshape(8, 64, 256)


def solution(mesh):
    in_specs = (
        P("tensor", "dp", "section"),
        P(),
        P(),
        P(("section", "dp"), "tensor", None),
        P(("section", "dp"), "tensor"),
        P("section", "tensor"),
        P("tensor", None, None),
        P(None, "tensor"),
        P("tensor"),
        P("tensor"),
        P("tensor"),
        P("tensor", None),
        P("tensor", None, ("section", "dp")),
    )
    out_specs = (
        P(None, "dp", "section"),
        P(("section", "dp"), "tensor", None),
        P("tensor", None, ("section", "dp")),
    )
    return jax.shard_map(
        per_device, mesh=mesh, in_specs=in_specs, out_specs=out_specs, check_vma=False
    )
```

```python
import jax
import jax.numpy as jnp
from jax import lax
from jax.experimental import pallas as pl
from jax.experimental.pallas import tpu as pltpu
from jax.sharding import PartitionSpec as P

STATE = 256
GROUP_HEADS = 32
KERNEL = 4
MESH = pl.DeviceIdType.MESH
NZ, NS, ND = 16, 8, 4
CHUNKS = 4
WIDTH = 1024 // CHUNKS
WHOLE = ((8,), (1, -1, 2, -2, 3, -3), (7, -7, 6, -6, 5, -5))
PIECES = ((), (4, -4), ())
VMEM = pl.BlockSpec(memory_space=pltpu.VMEM)
SMEM = pl.BlockSpec(memory_space=pltpu.SMEM)
HBM = pl.BlockSpec(memory_space=pltpu.HBM)
F32, BF16 = jnp.float32, jnp.bfloat16
ARRIVAL = (0, -1, 1, -2, 2, -3, 3, -4, 4, -5, 5, -6, 6, -7, 7, -8)


def place():
    return lax.axis_index("section"), lax.axis_index("tensor"), lax.axis_index("dp")


def turn(index, by, size):
    return lax.rem(index + (by % size), size)


def greet(peers):
    barrier = pltpu.get_barrier_semaphore()
    for peer in peers:
        pl.semaphore_signal(barrier, inc=1, device_id=peer, device_id_type=MESH)
    pl.semaphore_wait(barrier, len(peers))


def send(source, target, send_sem, recv_sem, peer):
    copy = pltpu.make_async_remote_copy(
        src_ref=source,
        dst_ref=target,
        send_sem=send_sem,
        recv_sem=recv_sem,
        device_id=peer,
        device_id_type=MESH,
    )
    copy.start()
    return copy


def dims(lhs, rhs):
    return (((lhs,), (rhs,)), ((), ()))


def layer_kernel(
    groups_ref, reads_ref, leaving_ref, origin_ref, scalars_ref,
    act_ref, xz_ref, dt_ref, bc_hbm, out_hbm, head_taps_hbm, gain_hbm,
    mixed_out, new_xz, new_rows,
    bc_ref, out_ref, head_taps_ref, gain_ref, load_sem,
    hot_ref, acts, weights, dts, rows_all, parts, parts_in, bc_parts, bc_in, step_parts, steps_in,
    bc_all, chosen, groups_in, xz_leaving, xz_coming, rows_leaving, rows_coming,
    own_gated, gathered, own_squares, squares_in, squares, z_squares, totals, product,
    right_out, right_in, left_out, left_in,
    w_send, w_recv, d_send, d_recv, o_send, o_recv, right_send, right_recv,
    left_send, left_recv, p_send, p_recv, b_send, b_recv, s_send, s_recv,
    z_send, z_recv, c_send, c_recv, e_send, e_recv, f_send, f_recv,
    g_send, g_recv, q_send, q_recv, u_send, u_recv, y_send, y_recv,
    sr_send, sr_recv, sl_send, sl_recv, gr_send, gr_recv, gl_send, gl_recv,
):
    s, t, d = place()
    right, left = (s, turn(t, 1, NZ), d), (s, turn(t, -1, NZ), d)
    sections = [turn(s, k, NS) for k in range(1, NS)]
    core = d + 1 - 2 * lax.rem(d, 2)
    across = turn(d, 2, ND)
    loads = [
        pltpu.make_async_copy(source, target, load_sem.at[i])
        for i, (source, target) in enumerate(
            (
                (out_hbm, out_ref),
                (bc_hbm, bc_ref),
                (head_taps_hbm, head_taps_ref),
                (gain_hbm, gain_ref),
            )
        )
    ]
    for load in loads:
        load.start()
    greet(
        [(s, turn(t, k, NZ), d) for k in range(1, NZ)]
        + [(p, t, d) for p in sections]
        + [(s, t, core), (s, t, across)]
    )
    sent = []

    def rows_at(index):
        return weights.at[pl.ds(pl.multiple_of(index * 256, 256), 256)]

    gathers = []

    def give(own, slot_of, ss, rs):
        near = send(own, slot_of(d), ss.at[0], rs.at[0], (s, t, core))
        far = send(own, slot_of(d), ss.at[1], rs.at[1], (s, t, across))
        sent.extend([near, far])
        gathers.append((slot_of, ss, rs, near, far))

    def start_ring(c):
        span = pl.ds(WIDTH * c, WIDTH)
        return [
            send(act_ref.at[:, span], acts.at[t, :, span], right_send.at[0, c], right_recv.at[0, c], right),
            send(act_ref.at[:, span], acts.at[t, :, span], left_send.at[0, c], left_recv.at[0, c], left),
        ]

    rings = [start_ring(c) for c in range(CHUNKS)]
    for ring in rings:
        sent.extend(ring)
    own_rows = pl.ds(pl.multiple_of(d * 256, 256), 256)
    for h in range(NS):
        weights[own_rows, 128 * h : 128 * h + 128] = xz_ref[h]
    give(rows_at(d), rows_at, w_send, w_recv)
    give(dt_ref, lambda i: dts.at[i], d_send, d_recv)
    acts[t] = act_ref[...]
    dts[d] = dt_ref[...]
    for load in loads:
        load.wait()
    rows_all[d] = out_ref[...].reshape(512, 256)
    lane = lax.broadcasted_iota(jnp.int32, (16, 128), 1)
    row = lax.rem(lax.broadcasted_iota(jnp.int32, (16, 128), 0), 8)
    halves = jnp.where(lane < 64, 0, 4)
    for h in range(NS):
        hot_ref[:, 128 * h : 128 * h + 128] = (row == halves + groups_ref[h]).astype(F32).astype(BF16)

    def pack(k):
        there = turn(t, k, NZ)
        if k == 0:
            xz_coming[t] = xz_ref[leaving_ref[there]]
            rows_coming[t] = out_ref[leaving_ref[there]]
        else:
            xz_leaving[k - 1] = xz_ref[leaving_ref[there]]
            rows_leaving[k - 1] = out_ref[leaving_ref[there]]

    for k in range(NZ):
        pack(k)
    moves = []

    def move(k, piece=None):
        there = (s, turn(t, k, NZ), d)
        parts_of = []
        if piece is None:
            parts_of.append((xz_leaving.at[k - 1], xz_coming.at[t], e_send.at[k - 1, 0], e_recv.at[k - 1, 0]))
            parts_of.append((rows_leaving.at[k - 1], rows_coming.at[t], f_send.at[k - 1, 0], f_recv.at[k - 1, 0]))
        elif piece < 4:
            rows = pl.ds(64 * piece, 64)
            parts_of.append(
                (xz_leaving.at[k - 1, rows], xz_coming.at[t, rows], e_send.at[k - 1, piece], e_recv.at[k - 1, piece])
            )
        else:
            half = piece - 4
            rows = pl.ds(32 * half, 32)
            parts_of.append(
                (rows_leaving.at[k - 1, rows], rows_coming.at[t, rows], f_send.at[k - 1, half], f_recv.at[k - 1, half])
            )
        for source, target, ss, rs in parts_of:
            copy = send(source, target, ss, rs, there)
            moves.append(copy)
            sent.append(copy)

    def move_whole(point):
        for k in WHOLE[point]:
            move(k % NZ)

    def move_pieces(ring, step):
        for k in PIECES[ring]:
            if step < 6:
                move(k % NZ, step)

    move_whole(0)
    forwarded = []

    def forward_weights(which):
        slot_of, ss, rs, near, far = gathers[which]
        far.wait_recv()
        copy = send(slot_of(across), slot_of(across), ss.at[2], rs.at[2], (s, t, core))
        forwarded.append(copy)
        sent.append(copy)

    def have_weights(which):
        gathers[which][3].wait_recv()
        forwarded[which].wait_recv()

    def block_of(i):
        return turn(t, ARRIVAL[i], NZ)

    part_copies = []

    def project(group):
        rows = jnp.concatenate([acts[block_of(4 * group + i)] for i in range(4)], axis=0)
        for half in range(2):
            result = jnp.dot(
                rows, weights[:, 512 * half : 512 * half + 512], preferred_element_type=F32
            ).astype(BF16)
            for j in range(4):
                parts[4 * half + j, 4 * group : 4 * group + 4] = result[
                    :, 128 * j : 128 * j + 128
                ].reshape(4, 64, 128)
        for k in range(1, NS):
            span = pl.ds(4 * group, 4)
            copy = send(
                parts.at[sections[k - 1], span],
                parts_in.at[k - 1, span],
                p_send.at[k - 1, group],
                p_recv.at[k - 1, group],
                (sections[k - 1], t, d),
            )
            part_copies.append(copy)
            sent.append(copy)

    for step in range(1, 9):
        for c in range(CHUNKS):
            span = pl.ds(WIDTH * c, WIDTH)
            rings[c][0].wait_recv()
            if step < 8:
                block = turn(t, -step, NZ)
                copy = send(
                    acts.at[block, :, span], acts.at[block, :, span],
                    right_send.at[step, c], right_recv.at[step, c], right,
                )
                rings[c][0] = copy
                sent.append(copy)
            if step < 8:
                rings[c][1].wait_recv()
            if step < 7:
                block = turn(t, step, NZ)
                copy = send(
                    acts.at[block, :, span], acts.at[block, :, span],
                    left_send.at[step, c], left_recv.at[step, c], left,
                )
                rings[c][1] = copy
                sent.append(copy)
        move_pieces(0, step - 1)
        if step == 3:
            forward_weights(0)
            forward_weights(1)
        if step == 4:
            have_weights(0)
            have_weights(1)
            project(0)
        if step == 5:
            project(1)

    bc_parts[0] = jnp.zeros((64, 128), BF16)
    for i in range(4):
        result = jnp.dot(
            acts[4 * i : 4 * i + 4].reshape(256, 1024), bc_ref[...], preferred_element_type=F32
        )
        bc_parts[1 + 4 * i : 5 + 4 * i] = result.astype(BF16).reshape(4, 64, 128)
    bc_copies = []
    for k in range(1, NS):
        copy = send(
            bc_parts.at[pl.ds(2 * sections[k - 1], 3)],
            bc_in.at[k - 1],
            b_send.at[k - 1],
            b_recv.at[k - 1],
            (sections[k - 1], t, d),
        )
        bc_copies.append(copy)
        sent.append(copy)
    move_whole(1)
    project(2)
    project(3)
    raw = jnp.zeros((16, 1024), F32)
    for i in range(ND):
        raw = raw + lax.dot_general(
            dts[i],
            acts[:, :, 256 * i : 256 * i + 256].reshape(1024, 256),
            dims(1, 1),
            preferred_element_type=F32,
        )
    for j in range(NS):
        for r in range(8):
            step_parts[j, r : r + 1, :] = raw[j : j + 1, 128 * r : 128 * r + 128]
    step_copies = []
    for k in range(1, NS):
        copy = send(
            step_parts.at[sections[k - 1]],
            steps_in.at[k - 1],
            s_send.at[k - 1],
            s_recv.at[k - 1],
            (sections[k - 1], t, d),
        )
        step_copies.append(copy)
        sent.append(copy)

    for copy in bc_copies:
        copy.wait_recv()
    total = bc_parts[pl.ds(2 * s, 3)].astype(F32)
    for k in range(NS - 1):
        total = total + bc_in[k].astype(F32)
    own_class, own_turn = 4 * lax.rem(t, 4), t // 4
    taps = dt_ref[8:16, 0:128].astype(F32)
    for m in range(2):
        rows = total[:, 32 * m : 32 * m + 32, :].reshape(96, 128)
        u = jnp.zeros((64, 128), F32)
        for k in range(KERNEL):
            u = u + taps[k : k + 1, :] * rows[29 + k : 93 + k]
        u = (u / (1.0 + jnp.exp(-u))).astype(BF16)
        bc_all[own_class + own_turn, 32 * m : 32 * m + 32, :] = u[:32]
        bc_all[own_class + own_turn, 64 + 32 * m : 96 + 32 * m, :] = u[32:]

    def spread(copies, source, slot, by):
        copy = send(source, source, z_send.at[slot], z_recv.at[slot], (s, turn(t, by, NZ), d))
        copies.append(copy)
        sent.append(copy)

    def gather_parts(start, stop):
        for i in range(start, stop):
            value = parts[s, i].astype(F32)
            for k in range(NS - 1):
                value = value + parts_in[k, i].astype(F32)
            product[block_of(i), :, 0:128] = value

    copies = []
    for slot, by in enumerate((4, -4, 8)):
        spread(copies, bc_all.at[own_class + own_turn], slot, by)
    for copy in part_copies[: 2 * NS - 2]:
        copy.wait_recv()
    gather_parts(0, 8)
    for copy in copies:
        copy.wait_recv()
    copies = []
    spread(copies, bc_all.at[pl.ds(own_class, 4)], 3, 1)
    spread(copies, bc_all.at[pl.ds(own_class, 4)], 4, -1)
    spread(copies, bc_all.at[own_class + own_turn], 5, 2)
    spread(copies, bc_all.at[own_class + turn(own_turn, 1, 4)], 6, 2)
    spread(copies, bc_all.at[own_class + turn(own_turn, 1, 4)], 7, -2)
    spread(copies, bc_all.at[own_class + turn(own_turn, 2, 4)], 8, -2)
    for copy in copies:
        copy.wait_recv()
    move_whole(2)

    def choose(section, j):
        return bc_all[reads_ref[4 * section + j]]

    choice_copies = []
    for k in range(1, NS):
        for j in range(4):
            chosen[k - 1, j] = choose(sections[k - 1], j)
        copy = send(
            chosen.at[k - 1], groups_in.at[s], c_send.at[k - 1], c_recv.at[k - 1],
            (sections[k - 1], t, d),
        )
        choice_copies.append(copy)
        sent.append(copy)
    for j in range(4):
        groups_in[s, j] = choose(s, j)
    give(rows_all.at[d], lambda i: rows_all.at[i], o_send, o_recv)

    for copy in part_copies[2 * NS - 2 :] + step_copies:
        copy.wait_recv()
    gather_parts(8, NZ)
    raw = step_parts[s]
    for k in range(NS - 1):
        raw = raw + steps_in[k]

    raw = jnp.concatenate(
        [
            jnp.concatenate(
                [raw[2 * c + i // 2 : 2 * c + i // 2 + 1, 64 * (i % 2) + 32 * m : 64 * (i % 2) + 32 * m + 32]
                 for i in range(4)],
                axis=1,
            )
            for m in range(2)
            for c in range(4)
        ],
        axis=0,
    )
    raw = raw + scalars_ref[8 + s]
    step = jnp.maximum(raw, 0.0) + jnp.log1p(jnp.exp(-jnp.abs(raw)))
    log_decay = -step * jnp.exp(jnp.full((8, 128), scalars_ref[s], F32))
    skip = scalars_ref[16 + s]
    taps = head_taps_ref[s].astype(F32)
    taps = jnp.concatenate([taps, taps], axis=1)
    lane = lax.broadcasted_iota(jnp.int32, (128, 128), 1)
    row = lax.broadcasted_iota(jnp.int32, (128, 128), 0)
    causal = row >= lane
    upto = (row <= lane).astype(F32)
    same = (row == lane).astype(F32)
    exact = lax.Precision.HIGHEST
    cum = jnp.dot(log_decay, upto, precision=exact, preferred_element_type=F32)
    both = jnp.concatenate([cum, step], axis=0)
    columns = lax.dot_general(same, both, dims(1, 1), precision=exact, preferred_element_type=F32)
    tall = lax.broadcasted_iota(jnp.int32, (512, 128), 0)
    for copy in choice_copies:
        copy.wait_recv()
    gated = []
    for m in range(2):
        v = product[:, 32 * m : 32 * m + 32, 0:128].reshape(512, 128)
        u = taps[3:4, :] * v
        for back in range(1, KERNEL):
            moved = jnp.where(tall >= back, pltpu.roll(v, back, 0), 0.0)
            u = u + taps[3 - back : 4 - back, :] * moved
        x = (u / (1.0 + jnp.exp(-u))).astype(BF16)
        state = jnp.zeros((STATE, 128), F32)
        outs = []
        for c in range(4):
            at = 4 * m + c

            def pick(j):
                part = groups_in[2 * c : 2 * c + 2, j].reshape(2, 2, 2, 32, 128)
                return part[:, :, m].reshape(128, 128)

            b = jnp.concatenate([pick(0), pick(1)], axis=1)
            cc = jnp.concatenate([pick(2), pick(3)], axis=1)
            xc = x[128 * c : 128 * c + 128]
            xf = xc.astype(F32)
            cum_c, step_c = columns[:, at : at + 1], columns[:, 8 + at : 9 + at]
            cum_r, step_r = cum[at : at + 1, :], step[at : at + 1, :]
            scores = lax.dot_general(cc, b, dims(1, 1), preferred_element_type=F32)
            mixing = jnp.exp(jnp.where(causal, cum_c - cum_r, -1e30)) * step_r
            y = jnp.dot((scores * mixing).astype(BF16), xc, preferred_element_type=F32)
            y = y + jnp.exp(cum_c) * jnp.dot(cc, state.astype(BF16), preferred_element_type=F32)
            y = y + skip * xf
            outs.append(y)
            if c < 3:
                end = cum[at : at + 1, 127:128]
                tail = (jnp.exp(end - cum_c) * step_c * xf).astype(BF16)
                state = jnp.exp(end) * state + lax.dot_general(
                    b, tail, dims(0, 0), preferred_element_type=F32
                )
        z = pltpu.roll(v, 64, 1)
        gated.append(jnp.concatenate(outs, axis=0) * (z / (1.0 + jnp.exp(-z))))
    wide = lax.broadcasted_iota(jnp.int32, (512, 128), 1)
    packed = jnp.where(wide < 64, gated[0], pltpu.roll(gated[1], 64, 1))
    own_gated[...] = packed.astype(BF16)

    y = lax.rem(s, 4)
    own_hot = hot_ref[:, pl.ds(pl.multiple_of(128 * s, 128), 128)]
    for j in range(4):
        part = packed[128 * j : 128 * j + 128]
        own_squares[j] = lax.dot_general(
            own_hot, (part * part).astype(BF16), dims(1, 1), preferred_element_type=F32
        )[:8]
    square_copies = []
    for k in range(1, NS):
        copy = send(
            own_squares.at[lax.rem(sections[k - 1], 4)], squares_in.at[k - 1],
            u_send.at[k - 1], u_recv.at[k - 1], (sections[k - 1], t, d),
        )
        square_copies.append(copy)
        sent.append(copy)
    gather_copies = []
    for k in range(1, NS):
        copy = send(
            own_gated, gathered.at[s], g_send.at[k - 1], g_recv.at[k - 1], (sections[k - 1], t, d)
        )
        gather_copies.append(copy)
        sent.append(copy)
    gathered[s] = own_gated[...]
    for copy in square_copies:
        copy.wait_recv()
    value = own_squares[y]
    for k in range(NS - 1):
        value = value + squares_in[k]
    squares[...] = value
    copies = []
    for k in range(1, NZ):
        copy = send(
            squares, z_squares.at[k - 1], q_send.at[k - 1], q_recv.at[k - 1],
            (s, turn(t, k, NZ), d),
        )
        copies.append(copy)
        sent.append(copy)
    for copy in copies:
        copy.wait_recv()
    for k in range(NZ - 1):
        value = value + z_squares[k]
    totals[y] = value
    copies = []
    for k in range(1, 4):
        copy = send(
            totals.at[y], totals.at[y], y_send.at[k - 1], y_recv.at[k - 1],
            (s - y + turn(y, k, 4), t, d),
        )
        copies.append(copy)
        sent.append(copy)
    forward_weights(2)
    for copy in copies + gather_copies:
        copy.wait_recv()
    have_weights(2)

    wide = lax.broadcasted_iota(jnp.int32, (128, 128), 1)
    gain = gain_ref[...].astype(F32)
    gain = jnp.concatenate([gain, gain], axis=1)

    def multiply(tile):
        inverse = lax.rsqrt(totals[tile] / (GROUP_HEADS * 64) + 1e-05)
        high = inverse.astype(BF16)
        low = (inverse - high.astype(F32)).astype(BF16)
        scale = lax.dot_general(
            jnp.concatenate([high, low], axis=0), hot_ref[...], dims(0, 0),
            preferred_element_type=F32,
        )
        first, second = [], []
        for i in range(0, NS, 2):
            pair = []
            for h in (i, i + 1):
                span = slice(128 * h, 128 * h + 128)
                value = gathered[h, pl.ds(pl.multiple_of(128 * tile, 128), 128), :].astype(F32)
                pair.append(value * scale[:, span] * gain[h : h + 1, :])
            even, odd = pair
            first.append(jnp.where(wide < 64, even, pltpu.roll(odd, 64, 1)).astype(BF16))
            second.append(jnp.where(wide < 64, pltpu.roll(even, 64, 1), odd).astype(BF16))
        lhs = jnp.concatenate(
            [jnp.concatenate(first, axis=1), jnp.concatenate(second, axis=1)], axis=0
        )
        for i in range(ND):
            result = jnp.dot(lhs, rows_all[i], preferred_element_type=F32)
            for m in range(2):
                product[
                    pl.ds(4 * tile, 4), 32 * m : 32 * m + 32, 256 * i : 256 * i + 256
                ] = result[128 * m : 128 * m + 128].reshape(4, 32, 256)

    first_tile = turn(t, 8, NZ) // 4
    for i in range(2):
        multiply(turn(first_tile, i, 4))

    from_left, from_right = [None] * CHUNKS, [None] * CHUNKS
    for step in range(8):
        if step == 1:
            for i in range(2, 4):
                multiply(turn(first_tile, i, 4))
        for h in range(CHUNKS):
            span = slice(WIDTH * h, WIDTH * h + WIDTH)
            value = product[turn(t, 8 - step, NZ), :, span]
            if step > 0:
                from_left[h].wait_recv()
                value = value + right_in[step - 1, h].astype(F32)
            right_out[step, h] = value.astype(BF16)
            from_left[h] = send(
                right_out.at[step, h], right_in.at[step, h],
                sr_send.at[step, h], sr_recv.at[step, h], right,
            )
            sent.append(from_left[h])
            if step < 7:
                value = product[turn(t, step - 7, NZ), :, span]
                if step > 0:
                    from_right[h].wait_recv()
                    value = value + left_in[step - 1, h].astype(F32)
                left_out[step, h] = value.astype(BF16)
                from_right[h] = send(
                    left_out.at[step, h], left_in.at[step, h],
                    sl_send.at[step, h], sl_recv.at[step, h], left,
                )
                sent.append(from_right[h])
        move_pieces(1, step)
    rings = []
    for h in range(CHUNKS):
        span = slice(WIDTH * h, WIDTH * h + WIDTH)
        from_left[h].wait_recv()
        from_right[h].wait_recv()
        value = product[t, :, span] + act_ref[:, span].astype(F32)
        value = value + right_in[7, h].astype(F32) + left_in[6, h].astype(F32)
        mixed_out[t, :, span] = value.astype(BF16)
        span = pl.ds(WIDTH * h, WIDTH)
        ring = []
        for ss, rs, peer in ((gr_send, gr_recv, right), (gl_send, gl_recv, left)):
            ring.append(
                send(mixed_out.at[t, :, span], mixed_out.at[t, :, span], ss.at[0, h], rs.at[0, h], peer)
            )
        sent.extend(ring)
        rings.append(ring)

    move_pieces(2, 0)
    for step in range(1, 9):
        for c in range(CHUNKS):
            span = pl.ds(WIDTH * c, WIDTH)
            rings[c][0].wait_recv()
            if step < 8:
                block = turn(t, -step, NZ)
                rings[c][0] = send(
                    mixed_out.at[block, :, span], mixed_out.at[block, :, span],
                    gr_send.at[step, c], gr_recv.at[step, c], right,
                )
                sent.append(rings[c][0])
            if step < 8:
                rings[c][1].wait_recv()
            if step < 7:
                block = turn(t, step, NZ)
                rings[c][1] = send(
                    mixed_out.at[block, :, span], mixed_out.at[block, :, span],
                    gl_send.at[step, c], gl_recv.at[step, c], left,
                )
                sent.append(rings[c][1])
        move_pieces(2, step)
        if step == 7:
            for copy in moves:
                copy.wait_recv()
            for k in range(NS):
                new_xz[:, 128 * k : 128 * k + 128] = xz_coming[origin_ref[k]]
                new_rows[64 * k : 64 * k + 64, :] = rows_coming[origin_ref[k]]
    for copy in sent:
        copy.wait_send()


def layer_call(*operands):
    def dma(*shape):
        return [pltpu.SemaphoreType.DMA(shape)] * 2

    return pl.pallas_call(
        layer_kernel,
        out_shape=(
            jax.ShapeDtypeStruct((NZ, 64, 1024), BF16),
            jax.ShapeDtypeStruct((256, 1024), BF16),
            jax.ShapeDtypeStruct((512, 256), BF16),
        ),
        in_specs=[SMEM] * 5 + [VMEM] * 3 + [HBM] * 4,
        out_specs=(VMEM,) * 3,
        scratch_shapes=[
            pltpu.VMEM((1024, 128), BF16),
            pltpu.VMEM((NS, 64, 256), BF16),
            pltpu.VMEM((NS, KERNEL, 64), BF16),
            pltpu.VMEM((NS, 64), BF16),
            pltpu.SemaphoreType.DMA((4,)),
            pltpu.VMEM((16, 1024), BF16),
            pltpu.VMEM((NZ, 64, 1024), BF16),
            pltpu.VMEM((1024, 1024), BF16),
            pltpu.VMEM((ND, 16, 256), BF16),
            pltpu.VMEM((ND, 512, 256), BF16),
            pltpu.VMEM((NS, NZ, 64, 128), BF16),
            pltpu.VMEM((NS - 1, NZ, 64, 128), BF16),
            pltpu.VMEM((NZ + 1, 64, 128), BF16),
            pltpu.VMEM((NS - 1, 3, 64, 128), BF16),
            pltpu.VMEM((NS, 8, 128), F32),
            pltpu.VMEM((NS - 1, 8, 128), F32),
            pltpu.VMEM((NZ, 128, 128), BF16),
            pltpu.VMEM((NS - 1, 4, 128, 128), BF16),
            pltpu.VMEM((NS, 4, 128, 128), BF16),
            pltpu.VMEM((NZ - 1, 256, 128), BF16),
            pltpu.VMEM((NZ, 256, 128), BF16),
            pltpu.VMEM((NZ - 1, 64, 256), BF16),
            pltpu.VMEM((NZ, 64, 256), BF16),
            pltpu.VMEM((512, 128), BF16),
            pltpu.VMEM((NS, 512, 128), BF16),
            pltpu.VMEM((4, 8, 128), F32),
            pltpu.VMEM((NS - 1, 8, 128), F32),
            pltpu.VMEM((8, 128), F32),
            pltpu.VMEM((NZ - 1, 8, 128), F32),
            pltpu.VMEM((4, 8, 128), F32),
            pltpu.VMEM((NZ, 64, 1024), F32),
            pltpu.VMEM((8, CHUNKS, 64, WIDTH), BF16),
            pltpu.VMEM((8, CHUNKS, 64, WIDTH), BF16),
            pltpu.VMEM((7, CHUNKS, 64, WIDTH), BF16),
            pltpu.VMEM((7, CHUNKS, 64, WIDTH), BF16),
            *dma(3), *dma(3), *dma(3),
            *dma(8, CHUNKS), *dma(7, CHUNKS),
            *dma(NS - 1, 4), *dma(NS - 1), *dma(NS - 1),
            *dma(9), *dma(NS - 1), *dma(NZ - 1, 4), *dma(NZ - 1, 2),
            *dma(NS - 1), *dma(NZ - 1), *dma(NS - 1), *dma(3),
            *dma(8, CHUNKS), *dma(7, CHUNKS), *dma(8, CHUNKS), *dma(7, CHUNKS),
        ],
        compiler_params=pltpu.CompilerParams(
            collective_id=0, has_side_effects=True, vmem_limit_bytes=36 << 20
        ),
        cost_estimate=pl.CostEstimate(
            flops=4_000_000_000, bytes_accessed=100_000_000, transcendentals=0
        ),
    )(*operands)


def head_maps(old_heads, new_heads, member):
    both = lax.optimization_barrier(jnp.stack([old_heads, new_heads]))
    mine = lax.dynamic_slice_in_dim(both, member * NS, NS, 1)
    groups = mine[0] // GROUP_HEADS
    j = jnp.arange(4, dtype=jnp.int32)
    block = 8 * (j // 2) + 2 * groups[:, None] + j % 2
    reads = (4 * (block % 4) + block // 4).reshape(4 * NS)
    slots = jnp.arange(NS, dtype=jnp.int32)
    owner = jnp.arange(NZ * NS, dtype=jnp.int32) // NS
    there = owner == jnp.arange(NZ, dtype=jnp.int32)[:, None]
    moved = both[1][:, None] == mine[0]
    leaving = jnp.sum(
        jnp.where(there[:, :, None] & moved, slots, 0), axis=(1, 2), dtype=jnp.int32
    )
    origin = jnp.sum(
        jnp.where(both[0] == mine[1][:, None], owner, 0), axis=1, dtype=jnp.int32
    )
    return groups, reads, leaving, origin


def per_device(
    activations,
    old_heads,
    new_heads,
    xz_weight,
    dt_weight,
    bc_weight,
    conv_heads,
    conv_groups,
    decay_log,
    dt_bias,
    skip_gain,
    norm_gain,
    out_weight,
):
    _, t, _ = place()
    groups, reads, leaving, origin = head_maps(old_heads, new_heads, t)
    mixed, new_xz, new_out = layer_call(
        groups,
        reads,
        leaving,
        origin,
        jnp.concatenate([decay_log, dt_bias, skip_gain]).astype(F32),
        jnp.transpose(activations, (1, 0, 2)).reshape(64, 1024),
        jnp.transpose(xz_weight, (1, 0, 2)),
        jnp.concatenate(
            [jnp.transpose(dt_weight), jnp.pad(conv_groups, ((0, 4), (0, 128)))], axis=0
        ),
        bc_weight,
        out_weight,
        conv_heads,
        norm_gain,
    )
    mixed = jnp.transpose(mixed.reshape(16, 2, 32, 1024), (0, 2, 1, 3)).reshape(512, 2, 1024)
    return mixed, new_xz.reshape(256, 8, 128), new_out.reshape(8, 64, 256)


def solution(mesh):
    in_specs = (
        P("tensor", "dp", "section"),
        P(),
        P(),
        P(("section", "dp"), "tensor", None),
        P(("section", "dp"), "tensor"),
        P("section", "tensor"),
        P("tensor", None, None),
        P(None, "tensor"),
        P("tensor"),
        P("tensor"),
        P("tensor"),
        P("tensor", None),
        P("tensor", None, ("section", "dp")),
    )
    out_specs = (
        P(None, "dp", "section"),
        P(("section", "dp"), "tensor", None),
        P("tensor", None, ("section", "dp")),
    )
    return jax.shard_map(
        per_device, mesh=mesh, in_specs=in_specs, out_specs=out_specs, check_vma=False
    )
```
